32 devices in a mesh: fsdp: 32 (over z, y, x, core).
Axes of the slice: x: 2, y: 2, z: 4, core: 2. Of those that a mesh axis runs over, the one named last changes fastest.
Arguments:
- tokens: bfloat16 [65536, 512], P('fsdp'), may hold values from -6 to 6
- seq_counts: int32 [32, 2], P('fsdp'), may hold values from 0 to 40, as said below
- returns: int32 [8192], P('fsdp'), may hold values from 1 to 11, as said below
- ln1_gain: bfloat16 [512], P('fsdp'), may hold values from 0.099609375 to 1.8984375
- qkv_weight: bfloat16 [512, 1536], P('fsdp'), may hold values from -0.25 to 0.25
- out_weight: bfloat16 [512, 512], P('fsdp'), may hold values from -0.75 to 0.75
- ln2_gain: bfloat16 [512], P('fsdp'), may hold values from 0.099609375 to 1.8984375
- up_weight: bfloat16 [512, 2048], P('fsdp'), may hold values from -0.25 to 0.25
- down_weight: bfloat16 [2048, 512], P('fsdp'), may hold values from -0.125 to 0.125
- prior_hidden_weight: bfloat16 [512, 512], P('fsdp'), may hold values from -0.25 to 0.25
- prior_logit_weight: bfloat16 [512, 1024], P('fsdp'), may hold values from -0.25 to 0.25
- frames_cot: bfloat16 [65536, 512], P('fsdp'), may hold values from -6 to 6
- logits_cot: bfloat16 [65536, 1024], P('fsdp'), may hold values from -6 to 6
Outputs:
- frames: bfloat16 [65536, 512], P('fsdp')
- logits: bfloat16 [65536, 1024], P('fsdp')
- tokens_grad: float32 [65536, 512], P('fsdp')
- ln1_gain_grad: float32 [512], P('fsdp')
- qkv_weight_grad: float32 [512, 1536], P('fsdp')
- out_weight_grad: float32 [512, 512], P('fsdp')
- ln2_gain_grad: float32 [512], P('fsdp')
- up_weight_grad: float32 [512, 2048], P('fsdp')
- down_weight_grad: float32 [2048, 512], P('fsdp')
- prior_hidden_weight_grad: float32 [512, 512], P('fsdp')
- prior_logit_weight_grad: float32 [512, 1024], P('fsdp')
The draws below stay inside these ranges and needn't reach their ends.
Inputs may be any that keep to these rules, and one draw needn't show every extreme that they name: `seq_counts`: column 0 counts a device's sequences of 64 frames and column 1 its sequences of 50 frames, with 64 * column 0 + 50 * column 1 <= 2048; in every draw one device holds 32 long sequences and another 2048 // 50 short ones and no long one. `returns`: whole numbers.
All inputs are finite; a program needn't handle non-finite values.
Results may differ from the reference program's by a relative error of at most 0.013.
Values may be sent and summed in bfloat16 or wider, within the bound.
A program may use at most 192 MiB of HBM per device.

```python
import math
import jax
import jax.numpy as jnp
from jax import lax

D = 512
HEAD_DIM = 64
FF = 2048
HEAD_HIDDEN = 512
LOGITS = 1024
LONG_LEN = 64
SHORT_LEN = 50
TOK_DEV = 2048
RET_DEV = 256
TOKENS = 65536
RETURNS = 8192
N_FSDP = 32


def draw_seq_counts(key, part):
    key = jax.random.fold_in(key, 11)
    first_key, second_key, pick_key, other_key = jax.random.split(key, 4)
    device = jnp.arange(N_FSDP, dtype=jnp.int32)
    long_most = TOK_DEV // LONG_LEN
    long_count = jax.random.randint(first_key, (N_FSDP,), 0, long_most + 1)
    room_left = (TOK_DEV - long_count * LONG_LEN) // SHORT_LEN
    short_count = jax.random.randint(second_key, (N_FSDP,), 0, room_left + 1)
    full_device = jax.random.randint(pick_key, (), 0, N_FSDP)
    empty_device = (full_device + 1 + jax.random.randint(other_key, (), 0, N_FSDP - 1)) % N_FSDP
    long_count = jnp.where(device == full_device, long_most, jnp.where(device == empty_device, 0, long_count))
    short_count = jnp.where(device == full_device, (TOK_DEV - long_most * LONG_LEN) // SHORT_LEN, jnp.where(device == empty_device, TOK_DEV // SHORT_LEN, short_count))
    return jnp.stack([long_count, short_count], axis=1).astype(jnp.int32)


def draw_returns(key, part):
    key = jax.random.fold_in(key, 23)
    position = jnp.arange(RETURNS, dtype=jnp.int32)
    device = position // RET_DEV
    ceiling = 3 + 8 * device // max(N_FSDP - 1, 1)
    drawn = jax.random.randint(key, (RETURNS,), 1, ceiling + 1)
    drawn = jnp.where(position == RETURNS - 1, 11, drawn)
    drawn = jnp.where(position == 0, 1, drawn)
    return drawn.astype(jnp.int32)


def shard_levels(own_key, shape, pieces, smallest, largest):
    loudness, own = 1.0, jax.random.fold_in(own_key, 6)
    for dim, blocks in pieces:
        heights = jnp.exp(jax.random.uniform(jax.random.fold_in(own, dim), (blocks,), jnp.float32, smallest / len(pieces), largest / len(pieces)))
        loudness = loudness * jnp.repeat(heights, shape[dim] // blocks).reshape([-1 if axis == dim else 1 for axis in range(len(shape))])
    return loudness


def noise(own_key, extent, width, limit, cuts=(), held_as=jnp.bfloat16):
    array = width * jax.random.normal(own_key, extent, jnp.float32)
    if cuts:
        array = array * shard_levels(own_key, extent, cuts, -0.22, 0.18)
    return jnp.clip(array, -limit, limit).astype(held_as)


def setup_inputs(seed: int = 0) -> dict:
    arg_keys = jax.random.split(jax.random.key(seed), 14)
    return {
        "tokens": noise(arg_keys[0], (TOKENS, D), 1.0, 6.0, ((0, 32),)),
        "seq_counts": draw_seq_counts(jax.random.fold_in(arg_keys[13], 71), 0),
        "returns": draw_returns(jax.random.fold_in(arg_keys[13], 71), 0),
        "ln1_gain": jnp.clip(1.0 + 0.18 * jax.random.normal(arg_keys[3], (D,), jnp.float32), 0.099609375, 1.8984375).astype(jnp.bfloat16),
        "qkv_weight": noise(arg_keys[4], (D, 3 * D), D ** -0.5, 0.25, ((0, 32),)),
        "out_weight": noise(arg_keys[5], (D, D), (D // 8) ** -0.5, 0.75, ((0, 32),)),
        "ln2_gain": jnp.clip(1.0 + 0.18 * jax.random.normal(arg_keys[6], (D,), jnp.float32), 0.099609375, 1.8984375).astype(jnp.bfloat16),
        "up_weight": noise(arg_keys[7], (D, FF), D ** -0.5, 0.25, ((0, 32),)),
        "down_weight": noise(arg_keys[8], (FF, D), FF ** -0.5, 0.125, ((0, 32),)),
        "prior_hidden_weight": noise(arg_keys[9], (D, HEAD_HIDDEN), D ** -0.5, 0.25, ((0, 32),)),
        "prior_logit_weight": noise(arg_keys[10], (HEAD_HIDDEN, LOGITS), HEAD_HIDDEN ** -0.5, 0.25, ((0, 32),)),
        "frames_cot": noise(arg_keys[11], (TOKENS, D), 1.0, 6.0, ((0, 32),)),
        "logits_cot": noise(arg_keys[12], (TOKENS, LOGITS), 1.0, 6.0, ((0, 32),)),
    }


@jax.custom_vjp
def low(v):
    return lax.optimization_barrier(v.astype(jnp.bfloat16)).astype(jnp.float32)

@jax.custom_vjp
def low_back(v):
    return v

def low_keep(v):
    return (low(v), None)

def low_pass(kept, grad):
    return (grad,)

def back_keep(v):
    return (v, None)

def back_low(kept, grad):
    return (low(grad),)
low.defvjp(low_keep, low_pass)
low_back.defvjp(back_keep, back_low)

def row_layout(counts, row_count):
    row_index = jnp.arange(row_count, dtype=jnp.int32)
    long_end = counts[0] * LONG_LEN
    short_end = long_end + counts[1] * SHORT_LEN
    in_short = long_end + (row_index - long_end) // SHORT_LEN * SHORT_LEN
    starts = jnp.where(row_index < long_end, row_index // LONG_LEN * LONG_LEN, jnp.where(row_index < short_end, in_short, row_index))
    return (starts.astype(jnp.int32), row_index < short_end)

def layer_norm(input_rows, norm_gain):
    centred = input_rows - lax.optimization_barrier(jnp.mean(input_rows, axis=-1, keepdims=True))
    spread = lax.optimization_barrier(jnp.mean(centred * centred, axis=-1, keepdims=True))
    return centred * lax.rsqrt(spread + 1e-05) * norm_gain

def product(left, right):
    return jnp.dot(left, right, preferred_element_type=jnp.float32, precision=lax.Precision.HIGHEST)

def device_rows(params, input_rows, starts):
    first_norm_gain, query_key_value_weight, w_out, second_norm_gain, up_projection_weight, w_down, w_hidden, w_logit = params
    row_count = input_rows.shape[0]
    head_count = D // HEAD_DIM
    attention_input = low(layer_norm(input_rows, first_norm_gain))
    qkv_rows = low(low_back(product(attention_input, query_key_value_weight)))
    query_rows = qkv_rows[:, :D].reshape(row_count, head_count, HEAD_DIM)
    key_rows = qkv_rows[:, D:2 * D].reshape(row_count, head_count, HEAD_DIM)
    value_rows = qkv_rows[:, 2 * D:].reshape(row_count, head_count, HEAD_DIM)
    raw_scores = jnp.einsum('qhd,khd->hqk', query_rows, key_rows, precision=lax.Precision.HIGHEST) * HEAD_DIM ** (-0.5)
    raw_scores = low_back(raw_scores)
    row_index = jnp.arange(row_count, dtype=jnp.int32)
    allowed = (row_index[None, :] >= starts[:, None]) & (row_index[None, :] <= row_index[:, None])
    scores = jnp.where(allowed[None], raw_scores, -1e+30)
    probs = low(jax.nn.softmax(scores, axis=-1))
    attended = jnp.einsum('hqk,khd->qhd', probs, value_rows, precision=lax.Precision.HIGHEST).reshape(row_count, D)
    attended = low(low_back(attended))
    residual_stream = input_rows + low_back(product(attended, w_out))
    feedforward_input = low(layer_norm(residual_stream, second_norm_gain))
    up_rows = low_back(product(feedforward_input, up_projection_weight))
    active = low(jax.nn.elu(up_rows))
    stream = residual_stream + low_back(product(active, w_down))
    head_in = low(stream)
    hidden = low_back(product(head_in, w_hidden))
    hidden_act = low(jax.nn.elu(hidden))
    logits = low_back(product(hidden_act, w_logit))
    return (stream, logits)

def return_scale(returns):
    return_table = returns.reshape(N_FSDP, RET_DEV).astype(jnp.float32)
    steps_back = RET_DEV - 1 - jnp.arange(RET_DEV, dtype=jnp.float32)
    decays = 0.01 * jnp.exp(steps_back * math.log(0.99))
    running = lax.optimization_barrier(jnp.sum(return_table * decays[None, :], axis=1))
    return jnp.sum(running) / N_FSDP

def reference(tokens, seq_counts, returns, ln1_gain, qkv_weight, out_weight, ln2_gain, up_weight, down_weight, prior_hidden_weight, prior_logit_weight, frames_cot, logits_cot):
    params = (ln1_gain.astype(jnp.float32), qkv_weight.astype(jnp.float32), out_weight.astype(jnp.float32), ln2_gain.astype(jnp.float32), up_weight.astype(jnp.float32), down_weight.astype(jnp.float32), prior_hidden_weight.astype(jnp.float32), prior_logit_weight.astype(jnp.float32))
    stacked = tokens.astype(jnp.float32).reshape(N_FSDP, TOK_DEV, D)
    starts, usable = jax.vmap(lambda counts: row_layout(counts, TOK_DEV))(seq_counts)

    def forward(weights, input_rows):
        blocked = jax.checkpoint(lambda element: device_rows(weights, element[0], element[1]))
        return lax.map(blocked, (input_rows, starts))
    (stream, logits), pullback = jax.vjp(forward, params, stacked)
    scale_total = return_scale(returns)
    live_rows = usable.astype(jnp.float32)[..., None]
    frame_back = frames_cot.astype(jnp.float32).reshape(N_FSDP, TOK_DEV, D) * live_rows
    logit_back = logits_cot.astype(jnp.float32).reshape(N_FSDP, TOK_DEV, LOGITS) * live_rows / scale_total
    weight_grads, token_grad = pullback((frame_back, logit_back))
    return (stream.reshape(TOKENS, D).astype(jnp.bfloat16), logits.reshape(TOKENS, LOGITS).astype(jnp.bfloat16), token_grad.reshape(TOKENS, D), weight_grads[0], weight_grads[1], weight_grads[2], weight_grads[3], weight_grads[4], weight_grads[5], weight_grads[6], weight_grads[7])
```

```python
import functools
import math

import jax
import jax.numpy as jnp
from jax import lax
from jax.experimental import pallas as pl
from jax.experimental.pallas import tpu as pltpu
from jax.sharding import PartitionSpec as P

HEAD_DIM = 64
LONG_LEN = 64
SHORT_LEN = 50
QB = 64
GROUP = 256
F32 = jnp.float32
BF16 = jnp.bfloat16
MESH = pl.DeviceIdType.MESH
VMEM_LIMIT = 63 * 2**20


def dot(left, right):
    return jnp.dot(left, right, preferred_element_type=F32)


def dot_t(left, right):
    return lax.dot_general(left, right, (((1,), (1,)), ((), ())), preferred_element_type=F32)


def t_dot(left, right):
    return lax.dot_general(left, right, (((0,), (0,)), ((), ())), preferred_element_type=F32)


def normalize(rows):
    centred = rows - jnp.mean(rows, axis=-1, keepdims=True)
    inv_std = lax.rsqrt(jnp.mean(centred * centred, axis=-1, keepdims=True) + 1e-05)
    return centred * inv_std, inv_std


def norm_back(grad, normed, inv_std, gain):
    scaled = grad * gain
    centre = jnp.mean(scaled, axis=-1, keepdims=True)
    slope = jnp.mean(scaled * normed, axis=-1, keepdims=True)
    return inv_std * (scaled - centre - normed * slope)


def column_sum(values):
    rows, width = values.shape
    return jnp.sum(values.reshape(rows // 8, 8, width), axis=0)


def gain_row(block, first):
    return jnp.concatenate([block[first + i : first + i + 1, :] for i in range(4)], axis=1)


def loop(count, body):
    lax.fori_loop(0, count, lambda i, c: (body(i), c)[1], 0)


class Place:
    def __init__(self, sizes):
        self.sizes = sizes
        self.me = lax.axis_index("fsdp")
        self.strides = [math.prod(sizes[d + 1 :]) for d in range(4)]
        self.digit = [lax.rem(self.me // self.strides[d], sizes[d]) for d in range(4)]

    def other(self, dim, k):
        return lax.rem(self.digit[dim] + k, self.sizes[dim])

    def device(self, dim, k):
        return self.me + (self.other(dim, k) - self.digit[dim]) * self.strides[dim]

    def barrier(self):
        barrier = pltpu.get_barrier_semaphore()
        count = 0
        for dim in range(4):
            for k in range(1, self.sizes[dim]):
                pl.semaphore_signal(
                    barrier, inc=1, device_id=(self.device(dim, k),), device_id_type=MESH
                )
                count += 1
        pl.semaphore_wait(barrier, count)


class Gather:
    def __init__(self, place, buf, send, recv, order):
        self.place, self.buf, self.send, self.recv = place, buf, send, recv
        self.order = tuple(order) + (3,)
        self.sent = []
        self.waiting = []

    def own(self):
        return self.buf.at[tuple(self.place.digit)]

    def launch(self, stage):
        place = self.place
        done = self.order[:stage]
        dim = self.order[stage]
        index = tuple(slice(None) if d in done else place.digit[d] for d in range(4))
        self.waiting = []
        slot = sum(place.sizes[d] - 1 for d in done)
        for k in range(1, place.sizes[dim]):
            block = self.buf.at[index]
            copy = pltpu.make_async_remote_copy(
                src_ref=block,
                dst_ref=block,
                send_sem=self.send.at[slot + k - 1],
                recv_sem=self.recv.at[slot + k - 1],
                device_id=(place.device(dim, k),),
                device_id_type=MESH,
            )
            copy.start()
            self.waiting.append(copy)
        self.sent += self.waiting

    def arrive(self):
        for copy in self.waiting:
            copy.wait_recv()
        self.waiting = []

    def step(self, stage):
        self.arrive()
        self.launch(stage)

    def finish(self):
        for copy in self.sent:
            copy.wait_send()


class Scatter:
    def __init__(self, place, src, slots, send, recv, order):
        self.place, self.src, self.slots = place, src, slots
        self.send, self.recv = send, recv
        self.order = (3,) + tuple(order[::-1])
        self.sent = []
        self.waiting = []

    def pick(self, stage, digit):
        dim = self.order[stage]
        left = [d for d in range(4) if d not in self.order[:stage]]
        index = tuple(digit if d == dim else slice(None) for d in left)
        base = self.src if stage == 0 else self.slots[stage - 1].at[0]
        return base.at[index]

    def launch(self, stage):
        place = self.place
        dim = self.order[stage]
        slot = sum(place.sizes[d] - 1 for d in self.order[:stage])
        self.waiting = []
        for k in range(1, place.sizes[dim]):
            copy = pltpu.make_async_remote_copy(
                src_ref=self.pick(stage, place.other(dim, k)),
                dst_ref=self.slots[stage].at[k - 1],
                send_sem=self.send.at[slot + k - 1],
                recv_sem=self.recv.at[slot + k - 1],
                device_id=(place.device(dim, k),),
                device_id_type=MESH,
            )
            copy.start()
            self.waiting.append(copy)
        self.sent += self.waiting

    def combine(self, stage, out=None):
        for copy in self.waiting:
            copy.wait_recv()
        self.waiting = []
        dim = self.order[stage]
        mine = self.pick(stage, self.place.digit[dim])
        slots = self.slots[stage]
        others = self.place.sizes[dim] - 1

        def add(index):
            total = mine[index].astype(F32)
            for k in range(others):
                total = total + slots[(k,) + index].astype(F32)
            return total

        if out is not None:
            out(add((Ellipsis,)))
            return

        def one(i):
            slots[0, i] = add((i,)).astype(BF16)

        loop(slots.shape[1], one)

    def step(self, stage):
        self.combine(stage - 1)
        self.launch(stage)

    def finish(self):
        for copy in self.sent:
            copy.wait_send()


def slot_shapes(sizes, order, rows, cols):
    shapes = []
    left = [0, 1, 2, 3]
    for dim in (3,) + tuple(order[::-1]):
        left.remove(dim)
        shapes.append((sizes[dim] - 1,) + tuple(sizes[d] for d in left) + (rows, cols))
    return shapes


def head_masks(value):
    row = lax.broadcasted_iota(jnp.int32, (4 * QB, GROUP), 0) // QB
    col = lax.broadcasted_iota(jnp.int32, (4 * QB, GROUP), 1) // HEAD_DIM
    return jnp.where(row == col, value, 0.0).astype(BF16)


def stack_heads(block, mask):
    return jnp.concatenate([block] * 4, axis=0) * mask


def pick_heads(stacked):
    col = lax.broadcasted_iota(jnp.int32, (QB, GROUP), 1) // HEAD_DIM
    parts = [stacked[h * QB : (h + 1) * QB] for h in range(4)]
    return jnp.where(
        col < 2,
        jnp.where(col == 0, parts[0], parts[1]),
        jnp.where(col == 2, parts[2], parts[3]),
    )


def score_bias(step, long_end, short_end):
    row = step * QB + lax.broadcasted_iota(jnp.int32, (QB, 2 * QB), 0)
    key = (step - 1) * QB + lax.broadcasted_iota(jnp.int32, (QB, 2 * QB), 1)
    past = (row - long_end).astype(F32)
    number = jnp.floor((past + 0.5) * (1.0 / SHORT_LEN)).astype(jnp.int32)
    begin = jnp.where(
        row < long_end,
        step * QB,
        jnp.where(row < short_end, long_end + number * SHORT_LEN, row),
    )
    return jnp.where((key >= begin) & (key <= row), 0.0, -1e30)


def attend_step(step, qkv_ref, probs_ref, att_ref, mask, long_end, short_end):
    bias = score_bias(step, long_end, short_end)
    bias = jnp.concatenate([bias] * 4, axis=0)
    now = pl.ds(pl.multiple_of(step * QB + QB, QB), QB)
    window = pl.ds(pl.multiple_of(step * QB, QB), 2 * QB)
    for g in range(2):
        base = 3 * GROUP * g
        query = stack_heads(qkv_ref[now, base : base + GROUP], mask)
        scores = dot_t(query, qkv_ref[window, base + GROUP : base + 2 * GROUP]) + bias
        top = jnp.max(scores, axis=-1, keepdims=True)
        weight = jnp.exp(scores - top)
        probs = (weight / jnp.sum(weight, axis=-1, keepdims=True)).astype(BF16)
        probs_ref[step, 4 * QB * g : 4 * QB * (g + 1), :] = probs
        out = dot(probs, qkv_ref[window, base + 2 * GROUP : base + 3 * GROUP])
        rows = pl.ds(pl.multiple_of(step * QB, QB), QB)
        att_ref[rows, GROUP * g : GROUP * (g + 1)] = pick_heads(out).astype(BF16)


def attend_back_step(step, qkv_ref, probs_ref, grad_ref, back_ref, carry_ref, mask, scaled_mask):
    now = pl.ds(pl.multiple_of(step * QB + QB, QB), QB)
    before = pl.ds(pl.multiple_of(step * QB, QB), QB)
    window = pl.ds(pl.multiple_of(step * QB, QB), 2 * QB)
    rows = pl.ds(pl.multiple_of(step * QB, QB), QB)
    for g in range(2):
        base = 3 * GROUP * g
        query = stack_heads(qkv_ref[now, base : base + GROUP], scaled_mask)
        keys = qkv_ref[window, base + GROUP : base + 2 * GROUP]
        values = qkv_ref[window, base + 2 * GROUP : base + 3 * GROUP]
        grad = stack_heads(grad_ref[rows, GROUP * g : GROUP * (g + 1)], mask)
        probs = probs_ref[step, 4 * QB * g : 4 * QB * (g + 1), :]
        wide = probs.astype(F32)
        prob_grad = dot_t(grad, values)
        inner = jnp.sum(wide * prob_grad, axis=-1, keepdims=True)
        score_grad = (wide * (prob_grad - inner)).astype(BF16)
        query_grad = pick_heads(dot(score_grad, keys)) * HEAD_DIM ** (-0.5)
        back_ref[now, base : base + GROUP] = query_grad.astype(BF16)
        for part, grads in ((1, t_dot(score_grad, query)), (2, t_dot(probs, grad))):
            held = carry_ref[2 * g + part - 1]
            cols = slice(base + part * GROUP, base + (part + 1) * GROUP)
            back_ref[before, cols] = (held + grads[:QB]).astype(BF16)
            carry_ref[2 * g + part - 1] = grads[QB:]


def forward_kernel(sizes, *refs):
    (
        counts, tokens, qkv_in, out_in, up_in, down_in, hid_in, logit_in, aux_in,
        qkv_hbm, probs_hbm, att_hbm, res_hbm, act_hbm, slope_hbm, frames_hbm,
        w_a, w_b, w_out, w_up, w_down, w_hid, w_logit, aux_out,
        norm_ref, qkv_ref, probs_ref, att_ref, res_ref, act_ref, slope_ref, frames_ref, mask_ref,
        *rest,
    ) = refs
    bufs, sends, recvs = rest[:8], rest[8:16], rest[16:24]
    out_sem = rest[24]
    out_copies = []

    def write_out(src, dst):
        copy = pltpu.make_async_copy(src, dst, out_sem.at[len(out_copies)])
        copy.start()
        out_copies.append(copy)

    place = Place(sizes)
    rows = tokens.shape[0]
    tile = 512
    tiles = rows // tile
    long_end = counts[0, 0] * LONG_LEN
    short_end = long_end + counts[0, 1] * SHORT_LEN

    xy, yx = (0, 2, 1), (0, 1, 2)
    orders = [xy, xy, yx, xy, xy, yx, yx, xy]
    items = [Gather(place, bufs[i], sends[i], recvs[i], orders[i]) for i in range(8)]
    aux, qkv_a, qkv_b, out_w, up_w, down_w, hid_w, logit_w = items

    place.barrier()
    own_sem = rest[25]
    own = [
        pltpu.make_async_copy(aux_in, aux.own(), own_sem.at[0]),
        pltpu.make_async_copy(out_in, out_w.own(), own_sem.at[1]),
        pltpu.make_async_copy(up_in, up_w.own(), own_sem.at[2]),
        pltpu.make_async_copy(down_in, down_w.own(), own_sem.at[3]),
        pltpu.make_async_copy(hid_in, hid_w.own(), own_sem.at[4]),
        pltpu.make_async_copy(logit_in, logit_w.own(), own_sem.at[5]),
    ]
    for g, item in ((0, qkv_a), (1, qkv_b)):
        for part in range(3):
            first = 2 * GROUP * part + GROUP * g
            own.append(
                pltpu.make_async_copy(
                    qkv_in.at[:, first : first + GROUP],
                    item.own().at[:, GROUP * part : GROUP * (part + 1)],
                    own_sem.at[6 + 3 * g + part],
                )
            )
    for copy in own:
        copy.start()
    for copy in own:
        copy.wait()

    aux.launch(0)
    qkv_a.launch(0)
    qkv_b.launch(0)
    mask_ref[...] = head_masks(HEAD_DIM ** (-0.5))
    qkv_ref[0:QB, :] = jnp.zeros((QB, qkv_ref.shape[1]), BF16)
    for stage in (1, 2, 3):
        aux.step(stage)
    aux.arrive()
    aux_sum = jnp.sum(bufs[0][...].reshape(-1, *bufs[0].shape[-2:]), axis=0)
    aux_out[...] = aux_sum
    gain_one = gain_row(aux_sum, 0)
    gain_two = gain_row(aux_sum, 4)

    def norm_tile(i):
        at = pl.ds(pl.multiple_of(i * tile, tile), tile)
        normed, _ = normalize(tokens[at, :].astype(F32))
        norm_ref[at, :] = (normed * gain_one).astype(BF16)

    qkv_a.step(1)
    qkv_b.step(1)
    out_w.launch(0)
    up_w.launch(0)
    loop(tiles, norm_tile)
    qkv_a.step(2)
    qkv_b.step(2)
    out_w.step(1)
    up_w.step(1)
    down_w.launch(0)

    for g, item in ((0, qkv_a), (1, qkv_b)):
        if g == 0:
            qkv_a.step(3)
            qkv_b.step(3)
        item.arrive()
        cols = slice(3 * GROUP * g, 3 * GROUP * (g + 1))

        def qkv_tile(i):
            at = pl.ds(pl.multiple_of(i * tile, tile), tile)
            to = pl.ds(pl.multiple_of(QB + i * tile, QB), tile)
            weight = bufs[1 + g][...].reshape(-1, 3 * GROUP)
            qkv_ref[to, cols] = dot(norm_ref[at, :], weight).astype(BF16)

        loop(tiles, qkv_tile)
    write_out(qkv_ref, qkv_hbm)
    write_out(bufs[1], w_a)
    write_out(bufs[2], w_b)

    steps = rows // QB

    def attend_some(part, parts):
        def one(i):
            attend_step(
                part * (steps // parts) + i, qkv_ref, probs_ref, att_ref, mask_ref[...], long_end, short_end
            )

        loop(steps // parts, one)

    out_w.step(2)
    up_w.step(2)
    down_w.step(1)
    hid_w.launch(0)
    attend_some(0, 4)
    out_w.step(3)
    up_w.step(3)
    down_w.step(2)
    logit_w.launch(0)
    attend_some(1, 4)
    hid_w.step(1)
    logit_w.step(1)
    attend_some(2, 4)
    down_w.step(3)
    hid_w.step(2)
    logit_w.step(2)
    attend_some(3, 4)
    hid_w.step(3)
    logit_w.step(3)
    write_out(probs_ref, probs_hbm)
    write_out(att_ref, att_hbm)
    out_w.arrive()
    up_w.arrive()

    def out_tile(i):
        at = pl.ds(pl.multiple_of(i * tile, tile), tile)
        weight = bufs[3][...].reshape(-1, bufs[3].shape[-1])
        residual = tokens[at, :].astype(F32) + dot(att_ref[at, :], weight)
        res_ref[at, :] = residual
        normed, _ = normalize(residual)
        norm_ref[at, :] = (normed * gain_two).astype(BF16)

    loop(tiles, out_tile)
    write_out(res_ref, res_hbm)
    write_out(bufs[3], w_out)

    def up_tile(i):
        at = pl.ds(pl.multiple_of(i * tile, tile), tile)
        weight = bufs[4][...].reshape(-1, bufs[4].shape[-1])
        half = weight.shape[1] // 2
        for c in range(2):
            cols = slice(c * half, (c + 1) * half)
            value = dot(norm_ref[at, :], weight[:, cols])
            slope = jnp.exp(jnp.minimum(value, 0.0))
            slope_ref[at, cols] = slope.astype(BF16)
            act_ref[at, cols] = jnp.where(value > 0, value, slope - 1.0).astype(BF16)

    loop(tiles, up_tile)
    write_out(act_ref, act_hbm)
    write_out(slope_ref, slope_hbm)
    write_out(bufs[4], w_up)
    down_w.arrive()

    def down_tile(i):
        at = pl.ds(pl.multiple_of(i * tile, tile), tile)
        weight = bufs[5][...].reshape(-1, bufs[5].shape[-1])
        frames_ref[at, :] = (res_ref[at, :] + dot(act_ref[at, :], weight)).astype(BF16)

    loop(tiles, down_tile)
    write_out(frames_ref, frames_hbm)
    write_out(bufs[5], w_down)
    hid_w.arrive()
    logit_w.arrive()
    write_out(bufs[6], w_hid)
    write_out(bufs[7], w_logit)
    for item in items:
        item.finish()
    for copy in out_copies:
        copy.wait()


def middle_kernel(
    counts, scale, frames, active, slope, residual, frames_cot, logits_cot,
    w_hid, w_logit, w_up, w_down, gain,
    logits, back, g_logit, g_hid, g_down, g_up, g_gain,
    sum_logit, sum_hid, sum_down, sum_up, sum_gain,
):
    step = pl.program_id(0)
    tile = frames.shape[0]
    sums = (sum_logit, sum_hid, sum_down, sum_up, sum_gain)

    @pl.when(step == 0)
    def _():
        for ref in sums:
            ref[...] = jnp.zeros_like(ref)

    live_end = counts[0, 0] * LONG_LEN + counts[0, 1] * SHORT_LEN
    row = step * tile + lax.broadcasted_iota(jnp.int32, (tile, 1), 0)
    live = jnp.where(row < live_end, 1.0, 0.0)
    inverse = 1.0 / scale[...]
    head_in = frames[...]
    hidden = dot(head_in, w_hid[...])
    hidden_slope = jnp.exp(jnp.minimum(hidden, 0.0))
    hidden_act = jnp.where(hidden > 0, hidden, hidden_slope - 1.0).astype(BF16)
    logits[...] = dot(hidden_act, w_logit[...]).astype(BF16)
    logit_back = (logits_cot[...].astype(F32) * (live * inverse)).astype(BF16)
    sum_logit[...] += t_dot(hidden_act, logit_back)
    hidden_back = (dot_t(logit_back, w_logit[...]) * hidden_slope).astype(BF16)
    sum_hid[...] += t_dot(head_in, hidden_back)
    stream_back = frames_cot[...].astype(F32) * live + dot_t(hidden_back, w_hid[...])
    down_back = stream_back.astype(BF16)
    normed, inv_std = normalize(residual[...])
    norm_in = (normed * gain[...]).astype(BF16)
    sum_down[...] += t_dot(active[...], down_back)
    up_back = (dot_t(down_back, w_down[...]) * slope[...].astype(F32)).astype(BF16)
    sum_up[...] += t_dot(norm_in, up_back)
    grad = dot_t(up_back, w_up[...])
    sum_gain[...] += column_sum(grad * normed)
    back[...] = stream_back + norm_back(grad, normed, inv_std, gain[...])

    @pl.when(step == pl.num_programs(0) - 1)
    def _():
        for out, ref in zip((g_logit, g_hid, g_down, g_up, g_gain), sums):
            out[...] = ref[...].astype(out.dtype)


def backward_kernel(sizes, *refs):
    (
        tokens, gain_one_in, gain_two_sum,
        back_hbm, att_hbm, qkv_hbm, probs_hbm, w_a_hbm, w_b_hbm, w_out_hbm,
        g_logit, g_hid, g_down, g_up,
        tokens_grad,
        o_qkv, o_out, o_up, o_down, o_hid, o_logit, o_gain,
        back_ref, att_ref, qkv_ref, probs_ref, w_a, w_b, w_out,
        norm_ref, grad_ref, qkvb_ref, carry_ref, mask_ref, g_a, g_b, g_out, aux_ref,
        *rest,
    ) = refs
    slots = [rest[4 * i : 4 * i + 4] for i in range(7)]
    rest = rest[28:]
    sends, recvs = rest[:7], rest[7:14]
    aux_send, aux_recv, in_sem, out_sem = rest[14:18]

    place = Place(sizes)
    rows = tokens.shape[0]
    tile = 512
    tiles = rows // tile
    steps = rows // QB

    loads = []
    for src, dst in (
        (back_hbm, back_ref), (w_out_hbm, w_out), (att_hbm, att_ref), (qkv_hbm, qkv_ref),
        (probs_hbm, probs_ref), (w_a_hbm, w_a), (w_b_hbm, w_b),
    ):
        copy = pltpu.make_async_copy(src, dst, in_sem.at[len(loads)])
        copy.start()
        loads.append(copy)

    xy, yx = (0, 2, 1), (0, 1, 2)
    srcs = [g_logit, g_hid, g_down, g_up, g_out, g_a, g_b]
    orders = [xy, yx, yx, xy, xy, xy, yx]
    items = [Scatter(place, srcs[i], slots[i], sends[i], recvs[i], orders[i]) for i in range(7)]
    logit_g, hid_g, down_g, up_g, out_g, a_g, b_g = items

    place.barrier()
    for item in (logit_g, hid_g, down_g, up_g):
        item.launch(0)

    gain_one = gain_one_in[...]
    mask_ref[0] = head_masks(1.0)
    mask_ref[1] = head_masks(HEAD_DIM ** (-0.5))
    carry_ref[...] = jnp.zeros_like(carry_ref)

    def norm_tile(i):
        at = pl.ds(pl.multiple_of(i * tile, tile), tile)
        normed, _ = normalize(tokens[at, :].astype(F32))
        norm_ref[at, :] = (normed * gain_one).astype(BF16)

    loop(tiles, norm_tile)
    logit_g.step(1)
    hid_g.step(1)
    for copy in loads[:3]:
        copy.wait()

    out_weight = w_out[...].reshape(-1, w_out.shape[-1])

    def out_tile(i):
        at = pl.ds(pl.multiple_of(i * tile, tile), tile)
        grad_ref[at, :] = dot_t(back_ref[at, :].astype(BF16), out_weight).astype(BF16)

    loop(tiles, out_tile)
    g_out[...] = t_dot(att_ref[...], back_ref[...].astype(BF16)).astype(BF16).reshape(g_out.shape)
    out_g.launch(0)
    down_g.step(1)
    up_g.step(1)
    for copy in loads[3:]:
        copy.wait()

    def attend_some(part, parts):
        def one(i):
            attend_back_step(
                part * (steps // parts) + i, qkv_ref, probs_ref, grad_ref, qkvb_ref, carry_ref, mask_ref[0], mask_ref[1]
            )

        loop(steps // parts, one)

    attend_some(0, 4)
    logit_g.step(2)
    hid_g.step(2)
    attend_some(1, 4)
    down_g.step(2)
    up_g.step(2)
    out_g.step(1)
    attend_some(2, 4)
    logit_g.step(3)
    hid_g.step(3)
    attend_some(3, 4)
    for g in range(2):
        for part in (1, 2):
            cols = slice(3 * GROUP * g + part * GROUP, 3 * GROUP * g + (part + 1) * GROUP)
            qkvb_ref[rows : rows + QB, cols] = carry_ref[2 * g + part - 1].astype(BF16)
    out_g.step(2)
    down_g.step(3)
    up_g.step(3)

    for g, ref, item in ((0, g_a, a_g), (1, g_b, b_g)):
        cols = slice(3 * GROUP * g, 3 * GROUP * (g + 1))
        grad = t_dot(norm_ref[...], qkvb_ref[QB:, cols])
        ref[...] = grad.astype(BF16).reshape(ref.shape)
        item.launch(0)
    out_g.step(3)

    weight_a = w_a[...].reshape(-1, w_a.shape[-1])
    weight_b = w_b[...].reshape(-1, w_b.shape[-1])
    half = 3 * GROUP
    aux_ref[0, 0:8, :] = jnp.zeros((8, aux_ref.shape[-1]), F32)

    def token_tile(i):
        at = pl.ds(pl.multiple_of(i * tile, tile), tile)
        to = pl.ds(pl.multiple_of(QB + i * tile, QB), tile)
        grad = dot_t(qkvb_ref[to, :half], weight_a) + dot_t(qkvb_ref[to, half:], weight_b)
        normed, inv_std = normalize(tokens[at, :].astype(F32))
        aux_ref[0, 0:8, :] += column_sum(grad * normed)
        back_ref[at, :] += norm_back(grad, normed, inv_std, gain_one)

    loop(tiles, token_tile)
    store = pltpu.make_async_copy(back_ref, tokens_grad, out_sem.at[0])
    store.start()
    a_g.step(1)
    b_g.step(1)

    aux_ref[0, 0:1, :] = jnp.sum(aux_ref[0, 0:8, :], axis=0, keepdims=True)
    aux_ref[0, 1:2, :] = jnp.sum(gain_two_sum[...], axis=0, keepdims=True)
    sent = []
    first = 1
    for dim in range(4):
        copies = []
        for k in range(1, sizes[dim]):
            copy = pltpu.make_async_remote_copy(
                src_ref=aux_ref.at[0],
                dst_ref=aux_ref.at[first + k - 1],
                send_sem=aux_send.at[first + k - 2],
                recv_sem=aux_recv.at[first + k - 2],
                device_id=(place.device(dim, k),),
                device_id_type=MESH,
            )
            copy.start()
            copies.append(copy)
        for copy in copies:
            copy.wait()
        total = aux_ref[0]
        for k in range(1, sizes[dim]):
            total = total + aux_ref[first + k - 1]
        aux_ref[0] = total
        first += sizes[dim] - 1
    o_gain[...] = aux_ref[0]

    a_g.step(2)
    b_g.step(2)

    def put(ref):
        def store_out(value):
            ref[...] = value

        return store_out

    logit_g.combine(3, put(o_logit))
    hid_g.combine(3, put(o_hid))
    down_g.combine(3, put(o_down))
    up_g.combine(3, put(o_up))
    out_g.combine(3, put(o_out))
    a_g.step(3)
    b_g.step(3)

    def put_group(g):
        def store_out(value):
            for part in range(3):
                first = 2 * GROUP * part + GROUP * g
                o_qkv[:, first : first + GROUP] = value[:, GROUP * part : GROUP * (part + 1)]

        return store_out

    a_g.combine(3, put_group(0))
    b_g.combine(3, put_group(1))
    for item in items:
        item.finish()
    store.wait()


def shape(dims, dtype):
    return jax.ShapeDtypeStruct(tuple(dims), dtype)


def grid_sizes(count):
    chips = count // 2
    return {16: (4, 2, 2, 2), 64: (4, 4, 4, 2)}.get(chips, (chips, 1, 1, 2))


def run_forward(sizes, counts, tokens, shards, aux):
    rows, width = tokens.shape
    qkv_w, out_w, up_w, down_w, hid_w, logit_w = shards
    blocks = [
        (aux.shape, F32),
        ((qkv_w.shape[0], 3 * GROUP), BF16),
        ((qkv_w.shape[0], 3 * GROUP), BF16),
        (out_w.shape, BF16),
        (up_w.shape, BF16),
        (down_w.shape, BF16),
        (hid_w.shape, BF16),
        (logit_w.shape, BF16),
    ]
    hidden = up_w.shape[1]
    whole = [shape(tuple(sizes) + tuple(b), t) for b, t in blocks]
    out_shape = [
        shape((rows + QB, 3 * width), BF16),
        shape((rows // QB, 8 * QB, 2 * QB), BF16),
        shape((rows, width), BF16),
        shape((rows, width), F32),
        shape((rows, hidden), BF16),
        shape((rows, hidden), BF16),
        shape((rows, width), BF16),
        *whole[1:],
        shape(aux.shape, F32),
    ]
    peers = sum(s - 1 for s in sizes)
    vmem = pl.BlockSpec(memory_space=pltpu.VMEM)
    any_space = pl.BlockSpec(memory_space=pl.ANY)
    return pl.pallas_call(
        functools.partial(forward_kernel, sizes),
        out_shape=out_shape,
        in_specs=[pl.BlockSpec(memory_space=pltpu.SMEM)] + [vmem] * 8,
        out_specs=[any_space] * 14 + [vmem],
        scratch_shapes=[
            pltpu.VMEM((rows, width), BF16),
            pltpu.VMEM((rows + QB, 3 * width), BF16),
            pltpu.VMEM((rows // QB, 8 * QB, 2 * QB), BF16),
            pltpu.VMEM((rows, width), BF16),
            pltpu.VMEM((rows, width), F32),
            pltpu.VMEM((rows, hidden), BF16),
            pltpu.VMEM((rows, hidden), BF16),
            pltpu.VMEM((rows, width), BF16),
            pltpu.VMEM((4 * QB, GROUP), BF16),
            *[pltpu.VMEM(w.shape, w.dtype) for w in whole],
            *[pltpu.SemaphoreType.DMA((peers,))] * 16,
            pltpu.SemaphoreType.DMA((14,)),
            pltpu.SemaphoreType.DMA((12,)),
        ],
        compiler_params=pltpu.CompilerParams(
            collective_id=0, has_side_effects=True, vmem_limit_bytes=VMEM_LIMIT
        ),
    )(counts, tokens, qkv_w, out_w, up_w, down_w, hid_w, logit_w, aux)


def run_middle(counts, scale, frames, active, slope, residual, frames_cot, logits_cot, weights, gain):
    rows, width = frames.shape
    hidden = active.shape[1]
    w_hid, w_logit, w_up, w_down = weights
    tile = 512

    def tiled(array):
        return pl.BlockSpec((tile, array.shape[1]), lambda i: (i, 0))

    def whole(dims):
        return pl.BlockSpec(tuple(dims), lambda i: (0, 0), pipeline_mode=pl.Buffered(1))

    grads = [w_logit.shape, w_hid.shape, w_down.shape, w_up.shape]
    return pl.pallas_call(
        middle_kernel,
        grid=(rows // tile,),
        in_specs=[
            pl.BlockSpec(memory_space=pltpu.SMEM),
            whole((1, 1)),
            *[tiled(a) for a in (frames, active, slope, residual, frames_cot, logits_cot)],
            *[whole(w.shape) for w in weights],
            whole((1, width)),
        ],
        out_specs=[
            tiled(logits_cot), tiled(residual), *[whole(g) for g in grads], whole((8, width)),
        ],
        out_shape=[
            shape(logits_cot.shape, BF16), shape(residual.shape, F32),
            *[shape(g, BF16) for g in grads], shape((8, width), F32),
        ],
        scratch_shapes=[pltpu.VMEM(g, F32) for g in grads] + [pltpu.VMEM((8, width), F32)],
        compiler_params=pltpu.CompilerParams(vmem_limit_bytes=VMEM_LIMIT),
    )(counts, scale, frames, active, slope, residual, frames_cot, logits_cot, *weights, gain)


def run_backward(sizes, tokens, gain_one, gain_two_sum, back, att, qkv, probs, w_a, w_b, w_out, grads, blocks):
    rows, width = tokens.shape
    g_logit, g_hid, g_down, g_up = grads
    xy, yx = (0, 2, 1), (0, 1, 2)
    kinds = [
        (blocks["logit"], xy), (blocks["hid"], yx), (blocks["down"], yx), (blocks["up"], xy),
        (blocks["out"], xy), (w_a.shape[-2:], xy), (w_b.shape[-2:], yx),
    ]
    slots = []
    for block, order in kinds:
        slots += [pltpu.VMEM(s, BF16) for s in slot_shapes(sizes, order, *block)]
    peers = sum(s - 1 for s in sizes)
    vmem = pl.BlockSpec(memory_space=pltpu.VMEM)
    any_space = pl.BlockSpec(memory_space=pl.ANY)
    return pl.pallas_call(
        functools.partial(backward_kernel, sizes),
        out_shape=[
            shape((rows, width), F32),
            shape((w_a.shape[-2], 3 * width), F32),
            shape(blocks["out"], F32), shape(blocks["up"], F32), shape(blocks["down"], F32),
            shape(blocks["hid"], F32), shape(blocks["logit"], F32),
            shape((8, width), F32),
        ],
        in_specs=[vmem] * 3 + [any_space] * 7 + [vmem] * 4,
        out_specs=[any_space] + [vmem] * 7,
        scratch_shapes=[
            pltpu.VMEM(back.shape, F32),
            pltpu.VMEM(att.shape, BF16),
            pltpu.VMEM(qkv.shape, BF16),
            pltpu.VMEM(probs.shape, BF16),
            pltpu.VMEM(w_a.shape, BF16),
            pltpu.VMEM(w_b.shape, BF16),
            pltpu.VMEM(w_out.shape, BF16),
            pltpu.VMEM((rows, width), BF16),
            pltpu.VMEM((rows, width), BF16),
            pltpu.VMEM(qkv.shape, BF16),
            pltpu.VMEM((4, QB, GROUP), F32),
            pltpu.VMEM((2, 4 * QB, GROUP), BF16),
            pltpu.VMEM(w_a.shape, BF16),
            pltpu.VMEM(w_b.shape, BF16),
            pltpu.VMEM(w_out.shape, BF16),
            pltpu.VMEM((1 + peers, 8, width), F32),
            *slots,
            *[pltpu.SemaphoreType.DMA((peers,))] * 16,
            pltpu.SemaphoreType.DMA((7,)),
            pltpu.SemaphoreType.DMA((1,)),
        ],
        compiler_params=pltpu.CompilerParams(
            collective_id=1, has_side_effects=True, vmem_limit_bytes=VMEM_LIMIT
        ),
    )(tokens, gain_one, gain_two_sum, back, att, qkv, probs, w_a, w_b, w_out, g_logit, g_hid, g_down, g_up)


def shards(
    sizes,
    tokens,
    seq_counts,
    returns,
    ln1_gain,
    qkv_weight,
    out_weight,
    ln2_gain,
    up_weight,
    down_weight,
    prior_hidden_weight,
    prior_logit_weight,
    frames_cot,
    logits_cot,
):
    count = math.prod(sizes)
    width = tokens.shape[1]
    me = lax.axis_index("fsdp")
    own = ln1_gain.shape[0]
    steps_back = returns.shape[0] - 1 - jnp.arange(returns.shape[0], dtype=F32)
    decays = 0.01 * jnp.exp(steps_back * math.log(0.99))
    local_mean = jnp.sum(returns.astype(F32) * decays)
    mine = (jnp.arange(width, dtype=jnp.int32) // own) == me
    spread = [
        jnp.where(mine, jnp.tile(gain.astype(F32), count), 0.0).reshape(4, 128)
        for gain in (ln1_gain, ln2_gain)
    ]
    aux = jnp.concatenate(spread + [jnp.full((8, 128), local_mean, F32)], axis=0)
    weights = (qkv_weight, out_weight, up_weight, down_weight, prior_hidden_weight, prior_logit_weight)
    (
        qkv, probs, att, residual, active, slope, frames,
        w_a, w_b, w_out, w_up, w_down, w_hid, w_logit, aux_sum,
    ) = run_forward(sizes, seq_counts, tokens, weights, aux)

    def flat(weight):
        return weight.reshape(-1, weight.shape[-1])

    gain_one = aux_sum[0:4].reshape(1, width)
    gain_two = aux_sum[4:8].reshape(1, width)
    scale = aux_sum[8:9, 0:1] / count
    logits, back, g_logit, g_hid, g_down, g_up, gain_two_sum = run_middle(
        seq_counts, scale, frames, active, slope, residual, frames_cot, logits_cot,
        tuple(flat(w) for w in (w_hid, w_logit, w_up, w_down)), gain_two,
    )
    blocks = {
        "out": out_weight.shape,
        "up": up_weight.shape,
        "down": down_weight.shape,
        "hid": prior_hidden_weight.shape,
        "logit": prior_logit_weight.shape,
    }

    def split(grad, block):
        return grad.reshape(tuple(sizes) + tuple(block))

    grads = (
        split(g_logit, blocks["logit"]),
        split(g_hid, blocks["hid"]),
        split(g_down, blocks["down"]),
        split(g_up, blocks["up"]),
    )
    tokens_grad, o_qkv, o_out, o_up, o_down, o_hid, o_logit, o_gain = run_backward(
        sizes, tokens, gain_one, gain_two_sum, back, att, qkv, probs, w_a, w_b, w_out, grads, blocks
    )
    gain_grads = lax.dynamic_slice_in_dim(o_gain[:2], me * own, own, 1)
    return (
        frames,
        logits,
        tokens_grad,
        gain_grads[0],
        o_qkv,
        o_out,
        gain_grads[1],
        o_up,
        o_down,
        o_hid,
        o_logit,
    )


def solution(mesh):
    sizes = grid_sizes(mesh.shape["fsdp"])
    row = P("fsdp", None)
    vector = P("fsdp")
    return jax.shard_map(
        functools.partial(shards, sizes),
        mesh=mesh,
        in_specs=(row, row, vector, vector, row, row, vector, row, row, row, row, row, row),
        out_specs=(row, row, row, vector, row, row, vector, row, row, row, row),
        check_vma=False,
    )
```

```python
import functools
import math

import jax
import jax.numpy as jnp
from jax import lax
from jax.experimental import pallas as pl
from jax.experimental.pallas import tpu as pltpu
from jax.sharding import PartitionSpec as P

HEAD_DIM = 64
LONG_LEN = 64
SHORT_LEN = 50
QB = 64
BATCH = 8
GROUP = 256
F32 = jnp.float32
BF16 = jnp.bfloat16
MESH = pl.DeviceIdType.MESH
VMEM_LIMIT = 63 * 2**20


def dot(left, right):
    return jnp.dot(left, right, preferred_element_type=F32)


def dot_t(left, right):
    return lax.dot_general(left, right, (((1,), (1,)), ((), ())), preferred_element_type=F32)


def t_dot(left, right):
    return lax.dot_general(left, right, (((0,), (0,)), ((), ())), preferred_element_type=F32)


def normalize(rows):
    centred = rows - jnp.mean(rows, axis=-1, keepdims=True)
    inv_std = lax.rsqrt(jnp.mean(centred * centred, axis=-1, keepdims=True) + 1e-05)
    return centred * inv_std, inv_std


def norm_back(grad, normed, inv_std, gain):
    scaled = grad * gain
    centre = jnp.mean(scaled, axis=-1, keepdims=True)
    slope = jnp.mean(scaled * normed, axis=-1, keepdims=True)
    return inv_std * (scaled - centre - normed * slope)


def gain_row(block, first):
    return jnp.concatenate([block[first + i : first + i + 1, :] for i in range(4)], axis=1)


def loop(count, body, hooks=()):
    def one(i, carry):
        body(i)
        for turn, hook in dict(hooks).items():
            pl.when(i == turn - 1)(hook)
        return carry

    lax.fori_loop(0, count, one, 0)


class Place:
    def __init__(self, sizes):
        self.sizes = sizes
        self.me = lax.axis_index("fsdp")
        self.strides = [math.prod(sizes[d + 1 :]) for d in range(4)]
        self.digit = [lax.rem(self.me // self.strides[d], sizes[d]) for d in range(4)]
        self.count = math.prod(sizes)
        self.others = [
            [lax.rem(self.digit[d] + k, sizes[d]) for k in range(sizes[d])] for d in range(4)
        ]
        self.devices = [
            [self.me + (other - self.digit[d]) * self.strides[d] for other in self.others[d]]
            for d in range(4)
        ]

    def barrier(self):
        barrier = pltpu.get_barrier_semaphore()
        count = 0
        for dim in range(4):
            for k in range(1, self.sizes[dim]):
                pl.semaphore_signal(
                    barrier, inc=1, device_id=(self.devices[dim][k],), device_id_type=MESH
                )
                count += 1
        pl.semaphore_wait(barrier, count)


class Transfer:
    def __init__(self, place, order, send, recv, half):
        self.place, self.order = place, order
        self.send, self.recv, self.half = send, recv, half
        self.pending = None

    def copies(self, stage):
        place, dim = self.place, self.order[stage]
        slot = sum(place.sizes[d] - 1 for d in self.order[:stage])
        for k in range(1, place.sizes[dim]):
            src, dst = self.ends(stage, k)
            yield pltpu.make_async_remote_copy(
                src_ref=src,
                dst_ref=dst,
                send_sem=self.send.at[self.half, slot + k - 1],
                recv_sem=self.recv.at[self.half, slot + k - 1],
                device_id=(place.devices[dim][k],),
                device_id_type=MESH,
            )

    def launch(self, stage):
        for copy in self.copies(stage):
            copy.start()
        self.pending = stage

    def arrive(self):
        if self.pending is not None:
            for copy in self.copies(self.pending):
                copy.wait_recv()
        self.pending = None

    def finish(self):
        for stage in range(4):
            for copy in self.copies(stage):
                copy.wait_send()


class GatherHalf(Transfer):
    def __init__(self, place, buf, cols, order, send, recv, half):
        super().__init__(place, tuple(order) + (3,), send, recv, half)
        self.buf, self.cols = buf, cols

    def ends(self, stage, k):
        done = self.order[:stage]
        index = tuple(slice(None) if d in done else self.place.digit[d] for d in range(4))
        block = self.buf.at[index + (slice(None), self.cols)]
        return block, block


class ScatterHalf(Transfer):
    def __init__(self, place, src, cols, slots, order, send, recv, half):
        super().__init__(place, (3,) + tuple(order[::-1]), send, recv, half)
        self.src, self.cols, self.slots = src, cols, slots

    def pick(self, stage, digit):
        left = [d for d in range(4) if d not in self.order[:stage]]
        index = tuple(digit if d == self.order[stage] else slice(None) for d in left)
        if stage == 0:
            return self.src.at[index + (slice(None), self.cols)]
        return self.slots[stage - 1].at[(0,) + index]

    def ends(self, stage, k):
        there = self.place.others[self.order[stage]][k]
        return self.pick(stage, there), self.slots[stage].at[k - 1]

    def total(self, stage, index):
        dim = self.order[stage]
        total = self.pick(stage, self.place.digit[dim])[index].astype(F32)
        for k in range(self.place.sizes[dim] - 1):
            total = total + self.slots[stage][(k,) + index].astype(F32)
        return total

    def combine(self, stage):
        self.arrive()
        slots = self.slots[stage]

        def one(i):
            slots[0, i] = self.total(stage, (i,)).astype(BF16)

        loop(slots.shape[1], one)

    def result(self):
        self.arrive()
        return self.total(3, (Ellipsis,))


ORDERS = ((0, 2, 1), (0, 1, 2))


def halves(width):
    return [slice(h * width // 2, (h + 1) * width // 2) for h in range(2)]


class Gather:
    def __init__(self, place, buf, send, recv):
        width = buf.shape[-1]
        parts = halves(width) if width >= 256 else [slice(0, width)]
        self.buf = buf
        self.parts = [
            GatherHalf(place, buf, cols, ORDERS[h], send, recv, h) for h, cols in enumerate(parts)
        ]
        self.own = buf.at[tuple(place.digit)]

    def step(self, stage):
        for part in self.parts:
            part.arrive()
            if stage < 4:
                part.launch(stage)

    def finish(self):
        for part in self.parts:
            part.finish()

    def whole(self):
        return self.buf[...].reshape(-1, self.buf.shape[-1])


class Scatter:
    def __init__(self, place, src, slots, send, recv):
        self.src = src
        self.cols = halves(src.shape[-1])
        self.parts = [
            ScatterHalf(place, src, self.cols[h], slots[4 * h : 4 * h + 4], ORDERS[h], send, recv, h)
            for h in range(2)
        ]

    def step(self, stage):
        for part in self.parts:
            if stage:
                part.combine(stage - 1)
            part.launch(stage)

    def put(self, out):
        for part, cols in zip(self.parts, self.cols):
            out(cols, part.result())

    def finish(self):
        for part in self.parts:
            part.finish()


def slot_shapes(sizes, rows, cols):
    shapes = []
    for order in ORDERS:
        left = [0, 1, 2, 3]
        for dim in (3,) + tuple(order[::-1]):
            left.remove(dim)
            shapes.append((sizes[dim] - 1,) + tuple(sizes[d] for d in left) + (rows, cols // 2))
    return shapes


def head_masks(value):
    row = lax.broadcasted_iota(jnp.int32, (4 * QB, GROUP), 0) // QB
    col = lax.broadcasted_iota(jnp.int32, (4 * QB, GROUP), 1) // HEAD_DIM
    return jnp.where(row == col, value, 0.0).astype(BF16)


def stack_heads(block, mask):
    return jnp.concatenate([block] * 4, axis=0) * mask


def pick_heads(stacked):
    col = lax.broadcasted_iota(jnp.int32, (QB, GROUP), 1) // HEAD_DIM
    parts = [stacked[h * QB : (h + 1) * QB] for h in range(4)]
    return jnp.where(
        col < 2,
        jnp.where(col == 0, parts[0], parts[1]),
        jnp.where(col == 2, parts[2], parts[3]),
    )


def score_bias(step, long_end, short_end):
    row = step * QB + lax.broadcasted_iota(jnp.int32, (QB, 2 * QB), 0)
    key = (step - 1) * QB + lax.broadcasted_iota(jnp.int32, (QB, 2 * QB), 1)
    past = (row - long_end).astype(F32)
    number = jnp.floor((past + 0.5) * (1.0 / SHORT_LEN)).astype(jnp.int32)
    begin = jnp.where(
        row < long_end,
        step * QB,
        jnp.where(row < short_end, long_end + number * SHORT_LEN, row),
    )
    return jnp.where((key >= begin) & (key <= row), 0.0, -1e30)


def row_block(step, count=1):
    return pl.ds(pl.multiple_of(step * QB, QB), count * QB)


def attend_steps(g, first, count, qkv_ref, probs_ref, att_ref, mask, long_end, short_end):
    base = 3 * GROUP * g
    work = []
    for step in [first + u for u in range(count)]:
        bias = score_bias(step, long_end, short_end)
        bias = jnp.concatenate([bias] * 4, axis=0)
        query = stack_heads(qkv_ref[row_block(step + 1), base : base + GROUP], mask)
        keys = qkv_ref[row_block(step, 2), base + GROUP : base + 2 * GROUP]
        work.append((step, dot_t(query, keys) + bias))
    done = []
    for step, scores in work:
        weight = jnp.exp(scores - jnp.max(scores, axis=-1, keepdims=True))
        total = jnp.sum(weight, axis=-1, keepdims=True)
        probs = (weight * pl.reciprocal(total)).astype(BF16)
        probs_ref[g, step] = probs
        done.append((step, probs))
    for step, probs in done:
        values = qkv_ref[row_block(step, 2), base + 2 * GROUP : base + 3 * GROUP]
        mixed = pick_heads(dot(probs, values))
        att_ref[row_block(step), GROUP * g : GROUP * (g + 1)] = mixed.astype(BF16)


def attend_back_steps(g, first, count, qkv_ref, probs_ref, grad_ref, back_ref, carry_ref, masks_ref):
    base = 3 * GROUP * g
    mask, scaled_mask = masks_ref[0], masks_ref[1]
    work = []
    for step in [first + u for u in range(count)]:
        query = stack_heads(qkv_ref[row_block(step + 1), base : base + GROUP], scaled_mask)
        keys = qkv_ref[row_block(step, 2), base + GROUP : base + 2 * GROUP]
        values = qkv_ref[row_block(step, 2), base + 2 * GROUP : base + 3 * GROUP]
        grad = stack_heads(grad_ref[row_block(step), GROUP * g : GROUP * (g + 1)], mask)
        work.append((step, query, keys, grad, dot_t(grad, values)))
    score_grads = []
    for step, _, _, _, prob_grad in work:
        probs = probs_ref[g, step].astype(F32)
        product = probs * prob_grad
        inner = jnp.sum(product, axis=-1, keepdims=True)
        score_grads.append((product - probs * inner).astype(BF16))
    held = [carry_ref[0], carry_ref[1]]
    for (step, query, keys, grad, _), score_grad in zip(work, score_grads):
        query_grad = pick_heads(dot(score_grad, keys)) * HEAD_DIM ** (-0.5)
        back_ref[row_block(step + 1), base : base + GROUP] = query_grad.astype(BF16)
        both = (t_dot(score_grad, query), t_dot(probs_ref[g, step], grad))
        for part, grads in enumerate(both):
            cols = slice(base + (part + 1) * GROUP, base + (part + 2) * GROUP)
            back_ref[row_block(step), cols] = (held[part] + grads[:QB]).astype(BF16)
            held[part] = grads[QB:]
    for part in range(2):
        carry_ref[part] = held[part]


def layer_kernel(sizes, *refs):
    (
        counts, gain_one_in, gain_two_in, returns_in,
        tokens_hbm, qkv_in, out_in, up_in, down_in, hid_in, logit_in, frames_cot, logits_cot,
        frames_hbm, act_hbm, logit_hbm, grad_hbm, qkv_hbm, probs_hbm,
        o_qkv, o_out, o_up, o_down, o_hid, o_logit, o_one, o_two,
        tokens, norm_ref, att_ref, back_ref, frames_ref, masks_ref, carry_ref, own_up, own_qkv,
        *rest,
    ) = refs
    bufs, rest = rest[:8], rest[8:]
    g_a, g_b, rest = rest[0], rest[1], rest[2:]
    slots, rest = [rest[8 * i : 8 * i + 8] for i in range(7)], rest[56:]
    g_sems, rest = [rest[2 * i : 2 * i + 2] for i in range(8)], rest[16:]
    s_sems, rest = [rest[2 * i : 2 * i + 2] for i in range(7)], rest[14:]
    own_sem, in_sem, out_sem, cot_sem, ha_sem = rest

    place = Place(sizes)
    rows, width = tokens.shape
    hidden = bufs[4].shape[-1]
    tile = 512
    tiles = rows // tile
    long_end = counts[0, 0] * LONG_LEN
    short_end = long_end + counts[0, 1] * SHORT_LEN

    def at(i, offset=0):
        return pl.ds(pl.multiple_of(offset + i * tile, QB), tile)

    def copy_in(src, dst, sem):
        copy = pltpu.make_async_copy(src, dst, sem)
        copy.start()
        return copy

    gathers = [Gather(place, bufs[i], *g_sems[i]) for i in range(8)]
    aux, qkv_a, qkv_b, out_w, up_w, down_w, hid_w, logit_w = gathers
    own = []
    for g, item in ((0, qkv_a), (1, qkv_b)):
        for part in range(3):
            first = 2 * GROUP * part + GROUP * g
            target = item.own.at[:, GROUP * part : GROUP * (part + 1)]
            own.append(copy_in(qkv_in.at[:, first : first + GROUP], target, own_sem.at[len(own)]))
    for src, item in ((out_in, out_w), (up_in, up_w), (down_in, down_w), (hid_in, hid_w), (logit_in, logit_w)):
        own.append(copy_in(src, item.own, own_sem.at[len(own)]))
    tokens_copy = copy_in(tokens_hbm, tokens, in_sem.at[0])
    late = [copy_in(up_in, own_up, in_sem.at[1]), copy_in(qkv_in, own_qkv, in_sem.at[2])]
    bufs[0][tuple(place.digit)] = own_block(place, gain_one_in, gain_two_in, returns_in)
    place.barrier()
    aux.step(0)
    for copy in own[:6]:
        copy.wait()
    qkv_a.step(0)
    qkv_b.step(0)
    for copy in own[6:]:
        copy.wait()
    masks_ref[0] = head_masks(1.0)
    masks_ref[1] = head_masks(HEAD_DIM ** (-0.5))
    aux.step(1)
    qkv_a.step(1)
    out_w.step(0)
    aux.step(2)
    qkv_b.step(1)
    up_w.step(0)
    qkv_a.step(2)
    aux.step(3)
    out_w.step(1)
    qkv_b.step(2)
    down_w.step(0)
    aux.step(4)
    aux_sum = jnp.sum(aux.buf[...].reshape(-1, *aux.buf.shape[-2:]), axis=0)
    gain_one = gain_row(aux_sum, 0)
    gain_two = gain_row(aux_sum, 4)
    inverse_scale = place.count / aux_sum[8:9, 0:1]
    tokens_copy.wait()

    def norm_tile(i):
        normed, _ = normalize(tokens[at(i), :].astype(F32))
        norm_ref[at(i), :] = (normed * gain_one).astype(BF16)

    loop(tiles, norm_tile, {2: lambda: qkv_a.step(3)})
    out_w.step(2)
    qkv_a.step(4)

    def start_all(*steps):
        def run():
            for item, stage in steps:
                item.step(stage)

        return run

    def qkv_phase(g, item, qkv_ref, hooks):
        cols = slice(3 * GROUP * g, 3 * GROUP * (g + 1))

        def one(i):
            qkv_ref[at(i, QB), cols] = dot(norm_ref[at(i), :], item.whole()).astype(BF16)

        loop(tiles, one, hooks)

    def attend_phase(g, qkv_ref, probs_ref, hooks):
        def one(i):
            attend_steps(g, i * BATCH, BATCH, qkv_ref, probs_ref, att_ref, masks_ref[1], long_end, short_end)

        loop(rows // QB // BATCH, one, hooks)

    def with_residual(res_ref):
        def attention(qkv_ref, probs_ref):
            qkv_ref[0:QB, :] = jnp.zeros((QB, qkv_ref.shape[1]), BF16)
            qkv_phase(0, qkv_a, qkv_ref, {1: start_all((qkv_b, 3)), 4: start_all((up_w, 1))})
            attend_phase(0, qkv_ref, probs_ref, {
                1: start_all((out_w, 3), (hid_w, 0)), 3: start_all((down_w, 1), (logit_w, 0)),
            })
            spills = [copy_in(probs_ref.at[0], probs_hbm.at[0], out_sem.at[0])]
            qkv_b.step(4)
            qkv_phase(1, qkv_b, qkv_ref, {1: start_all((up_w, 2))})
            spills.append(copy_in(qkv_ref, qkv_hbm, out_sem.at[1]))
            attend_phase(1, qkv_ref, probs_ref, {1: start_all((hid_w, 1)), 2: start_all((logit_w, 1), (down_w, 2))})
            spills.append(copy_in(probs_ref.at[1], probs_hbm.at[1], out_sem.at[2]))
            out_w.step(4)

            def out_tile(i):
                residual = tokens[at(i), :].astype(F32) + dot(att_ref[at(i), :], out_w.whole())
                res_ref[at(i), :] = residual
                normed, _ = normalize(residual)
                norm_ref[at(i), :] = (normed * gain_two).astype(BF16)

            loop(tiles, out_tile, {1: start_all((up_w, 3))})
            for copy in spills:
                copy.wait()

        pl.run_scoped(attention, pltpu.VMEM(qkv_hbm.shape, BF16), pltpu.VMEM(probs_hbm.shape, BF16))
        pl.run_scoped(
            functools.partial(feed_forward, res_ref),
            pltpu.VMEM((rows, hidden), BF16),
            pltpu.VMEM((rows, hidden), BF16),
            pltpu.VMEM((2, tile, frames_cot.shape[1]), BF16),
            pltpu.VMEM((2, tile, logits_cot.shape[1]), BF16),
            pltpu.VMEM((rows, width), BF16),
            pltpu.VMEM((width, logits_cot.shape[1]), F32),
            pltpu.VMEM((width, width), F32),
        )

    scatters = [
        Scatter(place, src, slots[i], *s_sems[i])
        for i, src in enumerate((bufs[7], bufs[6], bufs[5], bufs[4], bufs[3], g_a, g_b))
    ]
    logit_g, hid_g, down_g, up_g, out_g, a_g, b_g = scatters

    def feed_forward(res_ref, act_ref, slope_ref, fcot, lcot, ha_ref, sum_logit, sum_hid):
        def cotangents(i, slot):
            return [
                pltpu.make_async_copy(frames_cot.at[at(i), :], fcot.at[slot], cot_sem.at[0, slot]),
                pltpu.make_async_copy(logits_cot.at[at(i), :], lcot.at[slot], cot_sem.at[1, slot]),
            ]

        for copy in cotangents(0, 0):
            copy.start()
        up_w.step(4)

        def up_tile(i):
            for cols in halves(hidden):
                value = dot(norm_ref[at(i), :], up_w.whole()[:, cols])
                slope = jnp.exp(jnp.minimum(value, 0.0))
                slope_ref[at(i), cols] = slope.astype(BF16)
                act_ref[at(i), cols] = jnp.where(value > 0, value, slope - 1.0).astype(BF16)

        loop(tiles, up_tile, {1: start_all((hid_w, 2), (down_w, 3)), 2: start_all((logit_w, 2))})
        down_w.step(4)

        def frame_copy(i):
            return pltpu.make_async_copy(frames_ref.at[at(i), :], frames_hbm.at[at(i), :], ha_sem.at[0])

        def down_tile(i):
            value = res_ref[at(i), :] + dot(act_ref[at(i), :], down_w.whole())
            frames_ref[at(i), :] = value.astype(BF16)

        loop(tiles, down_tile, {1: start_all((hid_w, 3)), 2: start_all((logit_w, 3))})
        frames_copy = copy_in(frames_ref, frames_hbm, out_sem.at[3])
        hid_w.step(4)
        logit_w.step(4)
        logit_copy = copy_in(bufs[7], logit_hbm, out_sem.at[4])
        for item in gathers:
            item.finish()
        frames_copy.wait()
        sum_logit[...] = jnp.zeros_like(sum_logit)
        sum_hid[...] = jnp.zeros_like(sum_hid)

        def head_tile(i):
            slot = lax.rem(i, 2)

            @pl.when(i + 1 < tiles)
            def _():
                for copy in cotangents(i + 1, lax.rem(i + 1, 2)):
                    copy.start()

            for copy in cotangents(i, slot):
                copy.wait()
            row = i * tile + lax.broadcasted_iota(jnp.int32, (tile, 1), 0)
            live = jnp.where(row < short_end, 1.0, 0.0)
            head_in = frames_ref[at(i), :]
            hidden_rows = dot(head_in, hid_w.whole())
            slope = jnp.exp(jnp.minimum(hidden_rows, 0.0))
            hidden_act = jnp.where(hidden_rows > 0, hidden_rows, slope - 1.0).astype(BF16)
            ha_ref[at(i), :] = hidden_act
            logit_back = (lcot[slot].astype(F32) * (live * inverse_scale)).astype(BF16)
            sum_logit[...] += t_dot(hidden_act, logit_back)
            hidden_back = (dot_t(logit_back, logit_w.whole()) * slope).astype(BF16)
            sum_hid[...] += t_dot(head_in, hidden_back)
            stream_back = fcot[slot].astype(F32) * live + dot_t(hidden_back, hid_w.whole())
            back_ref[at(i), :] = stream_back
            frames_ref[at(i), :] = stream_back.astype(BF16)

        loop(tiles, head_tile)
        ha_copy = copy_in(ha_ref, act_hbm, out_sem.at[5])
        logit_copy.wait()
        bufs[7][...] = sum_logit[...].astype(BF16).reshape(bufs[7].shape)
        bufs[6][...] = sum_hid[...].astype(BF16).reshape(bufs[6].shape)
        logit_g.step(0)
        hid_g.step(0)

        def up_back_tile(i):
            for cols in halves(hidden):
                weight = down_w.whole()[cols]
                grad = dot_t(frames_ref[at(i), :], weight)
                slope_ref[at(i), cols] = (grad * slope_ref[at(i), cols].astype(F32)).astype(BF16)

        loop(tiles, up_back_tile, {2: start_all((logit_g, 1), (hid_g, 1))})

        chunk = hidden // sizes[0]

        def down_grad(i):
            cols = pl.ds(pl.multiple_of(i * chunk, chunk), chunk)
            grad = t_dot(act_ref[:, cols], frames_ref[...])
            bufs[5][i] = grad.astype(BF16).reshape(bufs[5].shape[1:])

        loop(sizes[0], down_grad, {3: start_all((logit_g, 2), (hid_g, 2))})
        down_g.step(0)

        def norm_back_tile(i):
            grad = dot_t(slope_ref[at(i), :], up_w.whole())
            normed, inv_std = normalize(res_ref[at(i), :])
            back_ref[at(i), :] += norm_back(grad, normed, inv_std, gain_two)

        loop(tiles, norm_back_tile, {1: start_all((logit_g, 3), (hid_g, 3)), 2: start_all((down_g, 1))})

        def up_grad(i):
            cols = pl.ds(pl.multiple_of(i * chunk, chunk), chunk)
            grad = t_dot(norm_ref[...], slope_ref[:, cols])
            bufs[4][:, :, :, :, :, cols] = grad.astype(BF16).reshape(bufs[4].shape[:-1] + (chunk,))

        loop(sizes[0], up_grad, {3: start_all((down_g, 2))})
        up_g.step(0)
        ha_copy.wait()

    pl.run_scoped(with_residual, pltpu.VMEM((rows, width), F32))

    def put(ref):
        def store_out(cols, value):
            ref[:, cols] = value

        return store_out

    def put_group(g):
        def store_out(cols, value):
            first = cols.start
            while first < cols.stop:
                last = min(cols.stop, (first // GROUP + 1) * GROUP)
                to = first // GROUP * 2 * GROUP + GROUP * g + first % GROUP
                o_qkv[:, to : to + last - first] = value[:, first - cols.start : last - cols.start]
                first = last

        return store_out

    def attention_back(qkv_ref, probs_ref, qkvb_ref):
        loads = [copy_in(qkv_hbm, qkv_ref, in_sem.at[3])]
        loads += [copy_in(probs_hbm.at[g], probs_ref.at[g], in_sem.at[4 + g]) for g in range(2)]

        def out_back_tile(i):
            out_back = back_ref[at(i), :].astype(BF16)
            frames_ref[at(i), :] = dot_t(out_back, out_w.whole()).astype(BF16)
            normed, _ = normalize(tokens[at(i), :].astype(F32))
            norm_ref[at(i), :] = (normed * gain_one).astype(BF16)

        loop(tiles, out_back_tile, {2: start_all((up_g, 1))})
        out_grad = t_dot(att_ref[...], back_ref[...].astype(BF16))
        bufs[3][...] = out_grad.astype(BF16).reshape(bufs[3].shape)
        out_g.step(0)
        for copy in loads:
            copy.wait()
        hooks = [
            {1: start_all((down_g, 3), (out_g, 1)), 2: start_all((up_g, 2))},
            {1: start_all((up_g, 3)), 2: start_all((a_g, 1)), 3: start_all((out_g, 3))},
        ]
        for g, ref, item in ((0, g_a, a_g), (1, g_b, b_g)):
            carry_ref[...] = jnp.zeros_like(carry_ref)

            def one(i):
                attend_back_steps(
                    g, i * BATCH, BATCH, qkv_ref, probs_ref, frames_ref, qkvb_ref, carry_ref, masks_ref
                )

            loop(rows // QB // BATCH, one, hooks[g])
            base = 3 * GROUP * g
            for part in range(2):
                cols = slice(base + (part + 1) * GROUP, base + (part + 2) * GROUP)
                qkvb_ref[rows : rows + QB, cols] = carry_ref[part].astype(BF16)
            grad = t_dot(norm_ref[...], qkvb_ref[QB:, base : base + 3 * GROUP])
            ref[...] = grad.astype(BF16).reshape(ref.shape)
            item.step(0)
            if g == 0:
                out_g.step(2)

        def token_tile(i):
            grad = dot_t(qkvb_ref[at(i, QB), : 3 * GROUP], qkv_a.whole())
            grad += dot_t(qkvb_ref[at(i, QB), 3 * GROUP :], qkv_b.whole())
            normed, inv_std = normalize(tokens[at(i), :].astype(F32))
            back_ref[at(i), :] += norm_back(grad, normed, inv_std, gain_one)

        loop(tiles, token_tile, {1: start_all((a_g, 2), (b_g, 1)), 4: start_all((a_g, 3), (b_g, 2))})

    pl.run_scoped(
        attention_back,
        pltpu.VMEM(qkv_hbm.shape, BF16),
        pltpu.VMEM(probs_hbm.shape, BF16),
        pltpu.VMEM(qkv_hbm.shape, BF16),
    )
    grad_copy = copy_in(back_ref, grad_hbm, out_sem.at[6])
    logit_g.put(put(o_logit))
    hid_g.put(put(o_hid))
    down_g.put(put(o_down))
    up_g.put(put(o_up))
    out_g.put(put(o_out))
    for copy in late:
        copy.wait()
    o_two[...] = gain_grad(o_up, own_up, gain_two_in)
    b_g.step(3)
    a_g.put(put_group(0))
    b_g.put(put_group(1))
    o_one[...] = gain_grad(o_qkv, own_qkv, gain_one_in)
    for item in scatters:
        item.finish()
    grad_copy.wait()


def own_block(place, gain_one, gain_two, returns):
    own = gain_one.shape[1]
    row = lax.broadcasted_iota(jnp.int32, (4, 128), 0)
    lane = lax.broadcasted_iota(jnp.int32, (4, 128), 1)
    mine = (row * 128 + lane) // own == place.me
    pick_row = lax.broadcasted_iota(jnp.int32, (own, 128), 0)
    pick_lane = lax.broadcasted_iota(jnp.int32, (own, 128), 1)
    pick = jnp.where(lax.rem(pick_lane, own) == pick_row, 1.0, 0.0).astype(BF16)
    spread = [
        jnp.where(mine, jnp.broadcast_to(dot(gain[...], pick), (4, 128)), 0.0)
        for gain in (gain_one, gain_two)
    ]
    time = lax.broadcasted_iota(jnp.int32, returns.shape, 0) * returns.shape[1]
    time = time + lax.broadcasted_iota(jnp.int32, returns.shape, 1)
    steps_back = (returns.shape[0] * returns.shape[1] - 1 - time).astype(F32)
    decays = 0.01 * jnp.exp(steps_back * math.log(0.99))
    terms = jnp.sum(returns[...].astype(F32) * decays, axis=0, keepdims=True)
    mean = jnp.sum(terms, axis=1, keepdims=True)
    return jnp.concatenate(spread + [jnp.broadcast_to(mean, (8, 128))], axis=0)


def gain_grad(weight_grad, weight, gain):
    product = weight_grad[...] * weight[...].astype(F32)
    ones = jnp.ones((8, product.shape[1]), F32)
    total = lax.dot_general(
        ones, product, (((1,), (1,)), ((), ())),
        precision=lax.Precision.HIGHEST, preferred_element_type=F32,
    )
    return total[0:1] / gain[...].astype(F32)


def shape(dims, dtype):
    return jax.ShapeDtypeStruct(tuple(dims), dtype)


def grid_sizes(count):
    chips = count // 2
    return {16: (4, 2, 2, 2), 64: (4, 4, 4, 2)}.get(chips, (chips, 1, 1, 2))


def run_layer(sizes, counts, gains, returns, tokens, weights, frames_cot, logits_cot):
    rows, width = tokens.shape
    qkv_w, out_w, up_w, down_w, hid_w, logit_w = weights
    group = (qkv_w.shape[0], 3 * GROUP)
    blocks = [group, group] + [w.shape for w in (out_w, up_w, down_w, hid_w, logit_w)]
    bufs = [shape(tuple(sizes) + (16, 128), F32)]
    bufs += [shape(tuple(sizes) + tuple(b), BF16) for b in blocks]
    scatter_blocks = [logit_w.shape, hid_w.shape, down_w.shape, up_w.shape, out_w.shape, group, group]
    slots = [s for block in scatter_blocks for s in slot_shapes(sizes, *block)]
    peers = sum(s - 1 for s in sizes)
    vmem = pl.BlockSpec(memory_space=pltpu.VMEM)
    any_space = pl.BlockSpec(memory_space=pl.ANY)
    own = gains[0].shape[1]
    return pl.pallas_call(
        functools.partial(layer_kernel, sizes),
        out_shape=[
            shape((rows, width), BF16),
            shape((rows, width), BF16),
            bufs[7],
            shape((rows, width), F32),
            shape((rows + QB, 3 * width), BF16),
            shape((2, rows // QB, 4 * QB, 2 * QB), BF16),
            *[shape(w.shape, F32) for w in weights],
            shape((1, own), F32),
            shape((1, own), F32),
        ],
        in_specs=[pl.BlockSpec(memory_space=pltpu.SMEM)] + [vmem] * 3 + [any_space] * 9,
        out_specs=[any_space] * 6 + [vmem] * 8,
        scratch_shapes=[
            pltpu.VMEM((rows, width), BF16),
            pltpu.VMEM((rows, width), BF16),
            pltpu.VMEM((rows, width), BF16),
            pltpu.VMEM((rows, width), F32),
            pltpu.VMEM((rows, width), BF16),
            pltpu.VMEM((2, 4 * QB, GROUP), BF16),
            pltpu.VMEM((2, QB, GROUP), F32),
            pltpu.VMEM(up_w.shape, BF16),
            pltpu.VMEM(qkv_w.shape, BF16),
            *[pltpu.VMEM(b.shape, b.dtype) for b in bufs],
            *[pltpu.VMEM(bufs[i].shape, BF16) for i in (1, 2)],
            *[pltpu.VMEM(s, BF16) for s in slots],
            *[pltpu.SemaphoreType.DMA((2, peers))] * 30,
            pltpu.SemaphoreType.DMA((11,)),
            pltpu.SemaphoreType.DMA((6,)),
            pltpu.SemaphoreType.DMA((7,)),
            pltpu.SemaphoreType.DMA((2, 2)),
            pltpu.SemaphoreType.DMA((1,)),
        ],
        compiler_params=pltpu.CompilerParams(
            collective_id=0, has_side_effects=True, vmem_limit_bytes=VMEM_LIMIT
        ),
    )(counts, *gains, returns, tokens, *weights, frames_cot, logits_cot)


def finish_kernel(act, weight, *refs):
    count = (len(refs) - 1) // 2
    refs[count][...] = dot(act[...], weight[...]).astype(BF16)
    for src, dst in zip(refs[:2], refs[count + 1 : count + 3]):
        dst[...] = src[...]

    @pl.when(pl.program_id(0) == 0)
    def _():
        for src, dst in zip(refs[2:count], refs[count + 3 :]):
            dst[...] = src[...]


def run_finish(act, weight, tall, small):
    rows, width = act.shape
    tile = 512

    def tiled(columns):
        return pl.BlockSpec((tile, columns), lambda i: (i, 0))

    def whole(array):
        return pl.BlockSpec(array.shape, lambda i: (0, 0))

    passed = [tiled(a.shape[1]) for a in tall] + [whole(a) for a in small]
    return pl.pallas_call(
        finish_kernel,
        grid=(rows // tile,),
        in_specs=[tiled(width), whole(weight), *passed],
        out_specs=[tiled(weight.shape[1]), *passed],
        out_shape=[shape((rows, weight.shape[1]), BF16), *[shape(a.shape, a.dtype) for a in tall + small]],
    )(act, weight, *tall, *small)


def shards(
    sizes,
    tokens,
    seq_counts,
    returns,
    ln1_gain,
    qkv_weight,
    out_weight,
    ln2_gain,
    up_weight,
    down_weight,
    prior_hidden_weight,
    prior_logit_weight,
    frames_cot,
    logits_cot,
):
    own = ln1_gain.shape[0]
    (
        frames, act, w_logit, tokens_grad, _, _,
        o_qkv, o_out, o_up, o_down, o_hid, o_logit, o_one, o_two,
    ) = run_layer(
        sizes, seq_counts, (ln1_gain.reshape(1, own), ln2_gain.reshape(1, own)), returns.reshape(-1, 128),
        tokens, (qkv_weight, out_weight, up_weight, down_weight, prior_hidden_weight, prior_logit_weight),
        frames_cot, logits_cot,
    )
    logits, frames, tokens_grad, o_qkv, o_out, o_up, o_down, o_hid, o_logit = run_finish(
        act, w_logit.reshape(-1, w_logit.shape[-1]),
        (frames, tokens_grad), (o_qkv, o_out, o_up, o_down, o_hid, o_logit),
    )
    return (
        frames, logits, tokens_grad, o_one.reshape(own), o_qkv, o_out, o_two.reshape(own),
        o_up, o_down, o_hid, o_logit,
    )


def solution(mesh):
    sizes = grid_sizes(mesh.shape["fsdp"])
    row = P("fsdp", None)
    vector = P("fsdp")
    return jax.shard_map(
        functools.partial(shards, sizes),
        mesh=mesh,
        in_specs=(row, row, vector, vector, row, row, vector, row, row, row, row, row, row),
        out_specs=(row, row, row, vector, row, row, vector, row, row, row, row),
        check_vma=False,
    )
```

```python
import functools
import math

import jax
import jax.numpy as jnp
from jax import lax
from jax.experimental import pallas as pl
from jax.experimental.pallas import tpu as pltpu
from jax.sharding import PartitionSpec as P

HEAD_DIM = 64
LONG_LEN = 64
SHORT_LEN = 50
QB = 64
BATCH = 8
GROUP = 256
F32 = jnp.float32
BF16 = jnp.bfloat16
MESH = pl.DeviceIdType.MESH
VMEM_LIMIT = 63 * 2**20


def dot(left, right):
    return jnp.dot(left, right, preferred_element_type=F32)


def dot_t(left, right):
    return lax.dot_general(left, right, (((1,), (1,)), ((), ())), preferred_element_type=F32)


def t_dot(left, right):
    return lax.dot_general(left, right, (((0,), (0,)), ((), ())), preferred_element_type=F32)


def normalize(rows):
    centred = rows - jnp.mean(rows, axis=-1, keepdims=True)
    inv_std = lax.rsqrt(jnp.mean(centred * centred, axis=-1, keepdims=True) + 1e-05)
    return centred * inv_std, inv_std


def norm_back(grad, normed, inv_std, gain):
    scaled = grad * gain
    centre = jnp.mean(scaled, axis=-1, keepdims=True)
    slope = jnp.mean(scaled * normed, axis=-1, keepdims=True)
    return inv_std * (scaled - centre - normed * slope)


def gain_row(block, first):
    return jnp.concatenate([block[first + i : first + i + 1, :] for i in range(4)], axis=1)


def loop(count, body, hooks=()):
    def one(i, carry):
        body(i)
        for turn, condition, hook in hooks:
            pl.when((i == turn - 1) & condition)(hook)
        return carry

    lax.fori_loop(0, count, one, 0)


class Place:
    def __init__(self, sizes):
        self.sizes = sizes
        self.me = lax.axis_index("fsdp")
        self.strides = [math.prod(sizes[d + 1 :]) for d in range(4)]
        self.digit = [lax.rem(self.me // self.strides[d], sizes[d]) for d in range(4)]
        self.count = math.prod(sizes)
        self.others = [
            [lax.rem(self.digit[d] + k, sizes[d]) for k in range(sizes[d])] for d in range(4)
        ]
        self.devices = [
            [self.me + (other - self.digit[d]) * self.strides[d] for other in self.others[d]]
            for d in range(4)
        ]

    def barrier(self):
        barrier = pltpu.get_barrier_semaphore()
        count = 0
        for dim in range(4):
            for k in range(1, self.sizes[dim]):
                pl.semaphore_signal(
                    barrier, inc=1, device_id=(self.devices[dim][k],), device_id_type=MESH
                )
                count += 1
        pl.semaphore_wait(barrier, count)


class Transfer:
    def __init__(self, place, order, send, recv, half):
        self.place, self.order = place, order
        self.send, self.recv, self.half = send, recv, half

    def copies(self, stage):
        place, dim = self.place, self.order[stage]
        slot = sum(place.sizes[d] - 1 for d in self.order[:stage])
        for k in range(1, place.sizes[dim]):
            src, dst = self.ends(stage, k)
            yield pltpu.make_async_remote_copy(
                src_ref=src,
                dst_ref=dst,
                send_sem=self.send.at[self.half, slot + k - 1],
                recv_sem=self.recv.at[self.half, slot + k - 1],
                device_id=(place.devices[dim][k],),
                device_id_type=MESH,
            )

    def launch(self, stage):
        for copy in self.copies(stage):
            copy.start()

    def arrive(self, stage):
        for copy in self.copies(stage):
            copy.wait_recv()

    def finish(self):
        for stage in range(4):
            for copy in self.copies(stage):
                copy.wait_send()


class GatherHalf(Transfer):
    def __init__(self, place, buf, cols, order, send, recv, half):
        super().__init__(place, tuple(order) + (3,), send, recv, half)
        self.buf, self.cols = buf, cols

    def ends(self, stage, k):
        done = self.order[:stage]
        index = tuple(slice(None) if d in done else self.place.digit[d] for d in range(4))
        block = self.buf.at[index + (slice(None), self.cols)]
        return block, block


class ScatterHalf(Transfer):
    def __init__(self, place, src, cols, slots, order, send, recv, half):
        super().__init__(place, (3,) + tuple(order[::-1]), send, recv, half)
        self.src, self.cols, self.slots = src, cols, slots

    def pick(self, stage, digit):
        left = [d for d in range(4) if d not in self.order[:stage]]
        index = tuple(digit if d == self.order[stage] else slice(None) for d in left)
        if stage == 0:
            return self.src.at[index + (slice(None), self.cols)]
        return self.slots[stage - 1].at[(0,) + index]

    def ends(self, stage, k):
        there = self.place.others[self.order[stage]][k]
        return self.pick(stage, there), self.slots[stage].at[k - 1]

    def total(self, stage, index):
        dim = self.order[stage]
        total = self.pick(stage, self.place.digit[dim])[index].astype(F32)
        for k in range(self.place.sizes[dim] - 1):
            total = total + self.slots[stage][(k,) + index].astype(F32)
        return total

    def combine(self, stage):
        self.arrive(stage)
        slots = self.slots[stage]

        def one(i):
            slots[0, i] = self.total(stage, (i,)).astype(BF16)

        loop(slots.shape[1], one)

    def result(self):
        self.arrive(3)
        return self.total(3, (Ellipsis,))


ORDERS = ((0, 2, 1), (0, 1, 2))


def halves(width, first=0):
    middle = first + width // 2
    return [slice(first, middle), slice(middle, first + width)]


class Gather:
    def __init__(self, place, buf, first, width, send, recv):
        parts = halves(width, first) if width >= 256 else [slice(0, width)]
        self.parts = [
            GatherHalf(place, buf, cols, ORDERS[h], send, recv, h) for h, cols in enumerate(parts)
        ]

    def step(self, stage):
        for part in self.parts:
            if stage:
                part.arrive(stage - 1)
            if stage < 4:
                part.launch(stage)

    def finish(self):
        for part in self.parts:
            part.finish()


class Scatter:
    def __init__(self, place, src, slots, send, recv, out):
        self.out = out
        self.cols = halves(src.shape[-1])
        self.parts = [
            ScatterHalf(place, src, self.cols[h], slots[4 * h : 4 * h + 4], ORDERS[h], send, recv, h)
            for h in range(2)
        ]

    def step(self, stage):
        for part, cols in zip(self.parts, self.cols):
            if stage == 4:
                self.out(cols, part.result())
                continue
            if stage:
                part.combine(stage - 1)
            part.launch(stage)

    def finish(self):
        for part in self.parts:
            part.finish()


def slot_shapes(sizes, rows, cols):
    shapes = []
    for order in ORDERS:
        left = [0, 1, 2, 3]
        for dim in (3,) + tuple(order[::-1]):
            left.remove(dim)
            shapes.append((sizes[dim] - 1,) + tuple(sizes[d] for d in left) + (rows, cols // 2))
    return shapes


def head_masks(value):
    row = lax.broadcasted_iota(jnp.int32, (4 * QB, GROUP), 0) // QB
    col = lax.broadcasted_iota(jnp.int32, (4 * QB, GROUP), 1) // HEAD_DIM
    return jnp.where(row == col, value, 0.0).astype(BF16)


def stack_heads(block, mask):
    return jnp.concatenate([block] * 4, axis=0) * mask


def pick_heads(stacked):
    col = lax.broadcasted_iota(jnp.int32, (QB, GROUP), 1) // HEAD_DIM
    parts = [stacked[h * QB : (h + 1) * QB] for h in range(4)]
    return jnp.where(
        col < 2,
        jnp.where(col == 0, parts[0], parts[1]),
        jnp.where(col == 2, parts[2], parts[3]),
    )


def score_bias(step, long_end, short_end):
    row = step * QB + lax.broadcasted_iota(jnp.int32, (QB, 2 * QB), 0)
    key = (step - 1) * QB + lax.broadcasted_iota(jnp.int32, (QB, 2 * QB), 1)
    past = (row - long_end).astype(F32)
    number = jnp.floor((past + 0.5) * (1.0 / SHORT_LEN)).astype(jnp.int32)
    begin = jnp.where(
        row < long_end,
        step * QB,
        jnp.where(row < short_end, long_end + number * SHORT_LEN, row),
    )
    return jnp.where((key >= begin) & (key <= row), 0.0, -1e30)


def row_block(step, count=1):
    return pl.ds(pl.multiple_of(step * QB, QB), count * QB)


def columns(i, size, offset=0):
    return pl.ds(pl.multiple_of(offset + i * size, 128), size)


def group_columns(g):
    return [columns(3 * g + part, GROUP) for part in range(3)]


def attend_steps(g, first, count, qkv_ref, probs_ref, att_ref, mask, long_end, short_end):
    query_cols, key_cols, value_cols = group_columns(g)
    work = []
    for step in [first + u for u in range(count)]:
        bias = score_bias(step, long_end, short_end)
        bias = jnp.concatenate([bias] * 4, axis=0)
        query = stack_heads(qkv_ref[row_block(step + 1), query_cols], mask)
        keys = qkv_ref[row_block(step, 2), key_cols]
        work.append((step, dot_t(query, keys) + bias))
    done = []
    for step, scores in work:
        weight = jnp.exp(scores - jnp.max(scores, axis=-1, keepdims=True))
        total = jnp.sum(weight, axis=-1, keepdims=True)
        probs = (weight * pl.reciprocal(total)).astype(BF16)
        probs_ref[g, step] = probs
        done.append((step, probs))
    for step, probs in done:
        values = qkv_ref[row_block(step, 2), value_cols]
        mixed = pick_heads(dot(probs, values))
        att_ref[row_block(step), columns(g, GROUP)] = mixed.astype(BF16)


def attend_back_steps(g, first, count, qkv_ref, probs_ref, grad_ref, back_ref, carry_ref, masks_ref):
    query_cols, key_cols, value_cols = group_columns(g)
    mask, scaled_mask = masks_ref[0], masks_ref[1]
    work = []
    for step in [first + u for u in range(count)]:
        query = stack_heads(qkv_ref[row_block(step + 1), query_cols], scaled_mask)
        keys = qkv_ref[row_block(step, 2), key_cols]
        values = qkv_ref[row_block(step, 2), value_cols]
        grad = stack_heads(grad_ref[row_block(step), columns(g, GROUP)], mask)
        work.append((step, query, keys, grad, dot_t(grad, values)))
    score_grads = []
    for step, _, _, _, prob_grad in work:
        probs = probs_ref[g, step].astype(F32)
        product = probs * prob_grad
        inner = jnp.sum(product, axis=-1, keepdims=True)
        score_grads.append((product - probs * inner).astype(BF16))
    held = [carry_ref[0], carry_ref[1]]
    for (step, query, keys, grad, _), score_grad in zip(work, score_grads):
        query_grad = pick_heads(dot(score_grad, keys)) * HEAD_DIM ** (-0.5)
        back_ref[row_block(step + 1), query_cols] = query_grad.astype(BF16)
        both = (t_dot(score_grad, query), t_dot(probs_ref[g, step], grad))
        for part, (cols, grads) in enumerate(zip((key_cols, value_cols), both)):
            back_ref[row_block(step), cols] = (held[part] + grads[:QB]).astype(BF16)
            held[part] = grads[QB:]
    for part in range(2):
        carry_ref[part] = held[part]


GATHER_PLAN = {
    "start": {0: ("aux0", "a0", "b0", "aux1", "out0", "a1", "up00", "aux2", "b1", "up10", "aux3", "a2", "out1", "aux4")},
    "norm": {1: ("down00", "b2"), 2: ("up01", "a3")},
    "qkv_a": {0: ("down10", "out2", "up11", "a4"), 3: ("b3",), 4: ("hid0",)},
    "attend_a": {1: ("up02", "down01"), 2: ("logit0",), 3: ("out3",), 4: ("down11",)},
    "qkv_b": {0: ("b4",), 1: ("up12",), 3: ("hid1",)},
    "attend_b": {1: ("up03",), 3: ("down02", "logit1")},
    "out": {0: ("out4",), 1: ("down12",)},
    "up": {0: ("up04",), 1: ("up13",), 2: ("hid2", "up14"), 3: ("down03",), 4: ("logit2",)},
    "down": {0: ("down04",), 2: ("down13", "hid3", "down14"), 4: ("logit3",)},
    "head": {0: ("hid4", "logit4")},
}
SCATTER_PLAN = {
    "sums": {0: ("logit0", "hid0")},
    "up_back": {1: ("logit1", "hid1")},
    "down_grad": {2: ("logit2",), 3: ("hid2",), 4: ("down0",)},
    "norm_back": {1: ("logit3", "hid3", "down1")},
    "up_grad": {2: ("down2", "up0")},
    "out_back": {1: ("logit4", "hid4"), 2: ("up1",)},
    "out_grad": {0: ("out0",)},
    "back_a": {1: ("out1", "down3")},
    "grad_a": {0: ("a0",)},
    "back_b": {1: ("up2",), 2: ("a1", "out2"), 4: ("down4",)},
    "grad_b": {0: ("up3", "b0")},
    "token": {1: ("a2", "out3"), 2: ("b1",)},
    "end": {0: ("b2", "a3", "out4", "up4", "b3", "a4", "b4")},
}


def layer_kernel(sizes, *refs):
    (
        counts, gain_one_in, gain_two_in, returns_in,
        tokens_hbm, qkv_in, out_in, up_in, down_in, hid_in, logit_in, frames_cot, logits_cot,
        frames_hbm, act_hbm, logit_hbm, grad_hbm, qkv_hbm, norm_hbm, inv_hbm,
        o_qkv, o_out, o_up, o_down, o_hid, o_logit, o_one, o_two,
        norm_ref, inv_ref, att_ref, back_ref, frames_ref, probs_ref, wide_a, wide_b,
        masks_ref, carry_ref, own_up, own_qkv,
        *rest,
    ) = refs
    bufs, rest = rest[:7], rest[7:]
    g_qkv, rest = rest[0], rest[1:]
    slots, rest = [rest[8 * i : 8 * i + 8] for i in range(7)], rest[56:]
    g_sems, rest = [rest[2 * i : 2 * i + 2] for i in range(10)], rest[20:]
    s_sems, rest = [rest[2 * i : 2 * i + 2] for i in range(7)], rest[14:]
    own_sem, in_sem, out_sem, cot_sem = rest
    aux_buf, qkv_buf, out_buf, up_buf, down_buf, hid_buf, logit_buf = bufs

    place = Place(sizes)
    rows, width = back_ref.shape
    hidden = up_buf.shape[-1]
    three = 3 * width
    tile = 512
    tall = 1024
    long_end = counts[0, 0] * LONG_LEN
    short_end = long_end + counts[0, 1] * SHORT_LEN

    def at(i, size=tile, offset=0):
        return pl.ds(pl.multiple_of(offset + i * size, QB), size)

    def start(src, dst, sem):
        copy = pltpu.make_async_copy(src, dst, sem)
        copy.start()
        return copy

    def whole(buf):
        return buf[...].reshape(-1, buf.shape[-1])

    def put(ref):
        def store_out(cols, value):
            ref[:, cols] = value

        return store_out

    def put_group(g):
        def store_out(cols, value):
            first = cols.start
            while first < cols.stop:
                last = min(cols.stop, (first // GROUP + 1) * GROUP)
                to = first // GROUP * 2 * GROUP + GROUP * g + first % GROUP
                o_qkv[:, to : to + last - first] = value[:, first - cols.start : last - cols.start]
                first = last

        return store_out

    def buffers(*pairs):
        return {
            name: Gather(place, buf, first, cols, *g_sems[i])
            for i, (name, buf, first, cols) in enumerate(pairs)
        }

    gathers = buffers(
        ("aux", aux_buf, 0, 128),
        ("a", qkv_buf.at[0], 0, 3 * GROUP),
        ("b", qkv_buf.at[1], 0, 3 * GROUP),
        ("out", out_buf, 0, width),
        ("up0", up_buf, 0, hidden // 2),
        ("up1", up_buf, hidden // 2, hidden // 2),
        ("down0", down_buf, 0, width // 2),
        ("down1", down_buf, width // 2, width // 2),
        ("hid", hid_buf, 0, hid_buf.shape[-1]),
        ("logit", logit_buf, 0, logit_buf.shape[-1]),
    )
    scatters = {
        name: Scatter(place, src, slots[i], *s_sems[i], out)
        for i, (name, src, out) in enumerate((
            ("logit", logit_buf, put(o_logit)),
            ("hid", hid_buf, put(o_hid)),
            ("down", down_buf, put(o_down)),
            ("up", up_buf, put(o_up)),
            ("out", out_buf, put(o_out)),
            ("a", g_qkv.at[0], put_group(0)),
            ("b", g_qkv.at[1], put_group(1)),
        ))
    }

    def transfers(*phases, group=0):
        hooks = []
        for g, phase in enumerate(phases):
            turns = {}
            for plan, items in ((GATHER_PLAN, gathers), (SCATTER_PLAN, scatters)):
                for turn, steps in plan.get(phase, {}).items():
                    turns.setdefault(turn, []).extend((items[s[:-1]], int(s[-1])) for s in steps)

            def run(steps):
                for item, stage in steps:
                    item.step(stage)

            for turn, steps in turns.items():
                hook = functools.partial(run, steps)
                if turn:
                    hooks.append((turn, True if len(phases) == 1 else group == g, hook))
                elif len(phases) == 1:
                    hook()
                else:
                    pl.when(group == g)(hook)
        return hooks

    own = []
    for g in range(2):
        for part in range(3):
            first = 2 * GROUP * part + GROUP * g
            target = qkv_buf.at[(g, *place.digit, slice(None), slice(GROUP * part, GROUP * (part + 1)))]
            own.append(start(qkv_in.at[:, first : first + GROUP], target, own_sem.at[len(own)]))
    for src, buf in ((out_in, out_buf), (up_in, up_buf), (down_in, down_buf), (hid_in, hid_buf), (logit_in, logit_buf)):
        own.append(start(src, buf.at[tuple(place.digit)], own_sem.at[len(own)]))
    own.append(start(up_in, own_up, own_sem.at[11]))
    own.append(start(qkv_in, own_qkv, own_sem.at[12]))
    aux_buf[tuple(place.digit)] = own_block(place, gain_one_in, gain_two_in, returns_in)
    masks_ref[0] = head_masks(1.0)
    masks_ref[1] = head_masks(HEAD_DIM ** (-0.5))
    place.barrier()
    for copy in own:
        copy.wait()

    def gains():
        aux = jnp.sum(aux_buf[...].reshape(-1, *aux_buf.shape[-2:]), axis=0)
        return gain_row(aux, 0), gain_row(aux, 4), place.count / aux[8:9, 0:1]

    def norm_gradient(i, size, grad, gain):
        normed = norm_ref[at(i, size), :].astype(F32) * (1.0 / gain)
        back_ref[at(i, size), :] += norm_back(grad, normed, inv_ref[at(i, size), 0:1], gain)

    def forward(tokens):
        tokens_copy = start(tokens_hbm, tokens, in_sem.at[0])
        transfers("start")
        gain_one, gain_two, _ = gains()
        tokens_copy.wait()

        def norm_tile(i):
            normed, inv_std = normalize(tokens[at(i, tall), :].astype(F32))
            norm_ref[at(i, tall), :] = (normed * gain_one).astype(BF16)
            inv_ref[at(i, tall), :] = jnp.broadcast_to(inv_std, (tall, inv_ref.shape[1]))

        loop(rows // tall, norm_tile, transfers("norm"))
        start(norm_ref, norm_hbm, out_sem.at[6])
        start(inv_ref, inv_hbm, out_sem.at[7])
        wide_a[0:QB, 0:three] = jnp.zeros((QB, three), BF16)

        def group(g):
            hooks = transfers("qkv_a", "qkv_b", group=g)
            cols = columns(g, 3 * GROUP)

            def qkv_tile(i):
                weight = qkv_buf[g].reshape(width, -1)
                wide_a[at(i, offset=QB), cols] = dot(norm_ref[at(i), :], weight).astype(BF16)

            loop(rows // tile, qkv_tile, hooks)

            @pl.when(g == 1)
            def _():
                start(wide_a.at[:, 0:three], qkv_hbm, out_sem.at[0])

            def attend(i):
                attend_steps(g, i * BATCH, BATCH, wide_a, probs_ref, att_ref, masks_ref[1], long_end, short_end)

            loop(rows // QB // BATCH, attend, transfers("attend_a", "attend_b", group=g))

        loop(2, group)
        pltpu.make_async_copy(norm_ref, norm_hbm, out_sem.at[6]).wait()
        pltpu.make_async_copy(inv_ref, inv_hbm, out_sem.at[7]).wait()
        hooks = transfers("out")

        def out_tile(i):
            residual = tokens[at(i), :].astype(F32) + dot(att_ref[at(i), :], whole(out_buf))
            back_ref[at(i), :] = residual
            normed, inv_std = normalize(residual)
            norm_ref[at(i), :] = (normed * gain_two).astype(BF16)
            inv_ref[at(i), :] = jnp.broadcast_to(inv_std, (tile, inv_ref.shape[1]))

        loop(rows // tile, out_tile, hooks)

    pl.run_scoped(forward, pltpu.VMEM((rows, width), BF16))
    pltpu.make_async_copy(wide_a.at[:, 0:three], qkv_hbm, out_sem.at[0]).wait()

    def feed_forward(fcot, lcot, ha_ref, sum_logit, sum_hid):
        _, gain_two, inverse_scale = gains()

        def cotangents(i, slot):
            return [
                pltpu.make_async_copy(frames_cot.at[at(i), :], fcot.at[slot], cot_sem.at[0, slot]),
                pltpu.make_async_copy(logits_cot.at[at(i), :], lcot.at[slot], cot_sem.at[1, slot]),
            ]

        for copy in cotangents(0, 0):
            copy.start()
        hooks = transfers("up")

        def up_tile(i):
            rows_at = at(lax.rem(i, 2), tall)
            for part in range(2):
                cols = columns(2 * (i // 2) + part, hidden // 4)
                value = dot(norm_ref[rows_at, :], up_buf[..., cols].reshape(width, -1))
                slope = jnp.exp(jnp.minimum(value, 0.0))
                wide_b[rows_at, cols] = slope.astype(BF16)
                wide_a[rows_at, cols] = jnp.where(value > 0, value, slope - 1.0).astype(BF16)

        loop(2 * rows // tall, up_tile, hooks)
        hooks = transfers("down")

        def down_tile(i):
            rows_at = at(lax.rem(i, 2), tall)
            cols = columns(i // 2, width // 2)
            value = dot(wide_a[rows_at, 0:hidden], down_buf[..., cols].reshape(hidden, -1))
            frames_ref[rows_at, cols] = (back_ref[rows_at, cols] + value).astype(BF16)

        loop(2 * rows // tall, down_tile, hooks)
        frames_copy = start(frames_ref, frames_hbm, out_sem.at[1])
        transfers("head")
        logit_copy = start(logit_buf, logit_hbm, out_sem.at[8])
        for item in gathers.values():
            item.finish()
        sum_logit[...] = jnp.zeros_like(sum_logit)
        sum_hid[...] = jnp.zeros_like(sum_hid)
        frames_copy.wait()

        def head_tile(i):
            slot = lax.rem(i, 2)

            @pl.when(i + 1 < rows // tile)
            def _():
                for copy in cotangents(i + 1, lax.rem(i + 1, 2)):
                    copy.start()

            for copy in cotangents(i, slot):
                copy.wait()
            row = i * tile + lax.broadcasted_iota(jnp.int32, (tile, 1), 0)
            live = jnp.where(row < short_end, 1.0, 0.0)
            logit_back = (lcot[slot].astype(F32) * (live * inverse_scale)).astype(BF16)
            head_in = frames_ref[at(i), :]
            hidden_rows = dot(head_in, whole(hid_buf))
            act_back = dot_t(logit_back, whole(logit_buf))
            slope = jnp.exp(jnp.minimum(hidden_rows, 0.0))
            hidden_act = jnp.where(hidden_rows > 0, hidden_rows, slope - 1.0).astype(BF16)
            hidden_back = (act_back * slope).astype(BF16)
            ha_ref[at(i), :] = hidden_act
            sum_logit[...] += t_dot(hidden_act, logit_back)
            stream_back = fcot[slot].astype(F32) * live + dot_t(hidden_back, whole(hid_buf))
            sum_hid[...] += t_dot(head_in, hidden_back)
            back_ref[at(i), :] = stream_back
            frames_ref[at(i), :] = stream_back.astype(BF16)

        loop(rows // tile, head_tile)
        act_copy = start(ha_ref, act_hbm, out_sem.at[9])
        logit_copy.wait()
        logit_buf[...] = sum_logit[...].astype(BF16).reshape(logit_buf.shape)
        hid_buf[...] = sum_hid[...].astype(BF16).reshape(hid_buf.shape)
        transfers("sums")

        def up_back_tile(i):
            for part in range(4):
                cols = slice(part * hidden // 4, (part + 1) * hidden // 4)
                grad = dot_t(frames_ref[at(i, tall), :], whole(down_buf)[cols])
                slope = wide_b[at(i, tall), cols].astype(F32)
                wide_b[at(i, tall), cols] = (grad * slope).astype(BF16)

        loop(rows // tall, up_back_tile, transfers("up_back"))
        act_copy.wait()


        def down_grad(i):
            grad = t_dot(wide_a[0:rows, columns(i, hidden // sizes[0])], frames_ref[...])
            down_buf[i] = grad.astype(BF16).reshape(down_buf.shape[1:])

        loop(sizes[0], down_grad, transfers("down_grad"))
        start(qkv_hbm, wide_a.at[:, 0:three], in_sem.at[1])

        def norm_back_tile(i):
            grad = dot_t(wide_b[at(i, tall), 0:hidden], whole(up_buf))
            norm_gradient(i, tall, grad, gain_two)

        loop(rows // tall, norm_back_tile, transfers("norm_back"))

        def up_grad(i):
            cols = columns(i, hidden // 2)
            grad = t_dot(norm_ref[...], wide_b[0:rows, cols])
            up_buf[..., cols] = grad.astype(BF16).reshape(up_buf.shape[:-1] + (-1,))

        loop(2, up_grad, transfers("up_grad"))
        start(norm_hbm, norm_ref, in_sem.at[2])
        start(inv_hbm, inv_ref, in_sem.at[3])

    pl.run_scoped(
        feed_forward,
        pltpu.VMEM((2, tile, frames_cot.shape[1]), BF16),
        pltpu.VMEM((2, tile, logits_cot.shape[1]), BF16),
        pltpu.VMEM((rows, width), BF16),
        pltpu.VMEM((width, logits_cot.shape[1]), F32),
        pltpu.VMEM((width, width), F32),
    )

    gain_one, _, _ = gains()

    def out_back_tile(i):
        out_back = back_ref[at(i, tall), :].astype(BF16)
        frames_ref[at(i, tall), :] = dot_t(out_back, whole(out_buf)).astype(BF16)

    loop(rows // tall, out_back_tile, transfers("out_back"))
    grad = t_dot(att_ref[...], back_ref[...].astype(BF16))
    out_buf[...] = grad.astype(BF16).reshape(out_buf.shape)
    transfers("out_grad")
    pltpu.make_async_copy(qkv_hbm, wide_a.at[:, 0:three], in_sem.at[1]).wait()
    pltpu.make_async_copy(norm_hbm, norm_ref, in_sem.at[2]).wait()
    pltpu.make_async_copy(inv_hbm, inv_ref, in_sem.at[3]).wait()

    def group_back(g):
        carry_ref[...] = jnp.zeros_like(carry_ref)

        def attend_back(i):
            attend_back_steps(g, i * BATCH, BATCH, wide_a, probs_ref, frames_ref, wide_b, carry_ref, masks_ref)

        loop(rows // QB // BATCH, attend_back, transfers("back_a", "back_b", group=g))
        for part, cols in enumerate(group_columns(g)[1:]):
            wide_b[rows : rows + QB, cols] = carry_ref[part].astype(BF16)
        grad = t_dot(norm_ref[...], wide_b[QB : QB + rows, columns(g, 3 * GROUP)])
        g_qkv[g] = grad.astype(BF16).reshape(g_qkv.shape[1:])
        transfers("grad_a", "grad_b", group=g)

    loop(2, group_back)
    hooks = transfers("token")

    def token_tile(i):
        grad = dot_t(wide_b[at(i, offset=QB), 0 : 3 * GROUP], qkv_buf[0].reshape(width, -1))
        grad += dot_t(wide_b[at(i, offset=QB), 3 * GROUP : three], qkv_buf[1].reshape(width, -1))
        norm_gradient(i, tile, grad, gain_one)
        start(back_ref.at[at(i), :], grad_hbm.at[at(i), :], out_sem.at[2 + i])

    loop(rows // tile, token_tile, hooks)
    transfers("end")
    o_two[...] = gain_grad(o_up, own_up, gain_two_in)
    o_one[...] = gain_grad(o_qkv, own_qkv, gain_one_in)
    for item in scatters.values():
        item.finish()
    for i in range(rows // tile):
        pltpu.make_async_copy(back_ref.at[at(i), :], grad_hbm.at[at(i), :], out_sem.at[2 + i]).wait()


def own_block(place, gain_one, gain_two, returns):
    own = gain_one.shape[1]
    row = lax.broadcasted_iota(jnp.int32, (4, 128), 0)
    lane = lax.broadcasted_iota(jnp.int32, (4, 128), 1)
    mine = (row * 128 + lane) // own == place.me
    pick_row = lax.broadcasted_iota(jnp.int32, (own, 128), 0)
    pick_lane = lax.broadcasted_iota(jnp.int32, (own, 128), 1)
    pick = jnp.where(lax.rem(pick_lane, own) == pick_row, 1.0, 0.0).astype(BF16)
    spread = [
        jnp.where(mine, jnp.broadcast_to(dot(gain[...], pick), (4, 128)), 0.0)
        for gain in (gain_one, gain_two)
    ]
    time = lax.broadcasted_iota(jnp.int32, returns.shape, 0) * returns.shape[1]
    time = time + lax.broadcasted_iota(jnp.int32, returns.shape, 1)
    steps_back = (returns.shape[0] * returns.shape[1] - 1 - time).astype(F32)
    decays = 0.01 * jnp.exp(steps_back * math.log(0.99))
    terms = jnp.sum(returns[...].astype(F32) * decays, axis=0, keepdims=True)
    mean = jnp.sum(terms, axis=1, keepdims=True)
    return jnp.concatenate(spread + [jnp.broadcast_to(mean, (8, 128))], axis=0)


def gain_grad(weight_grad, weight, gain):
    product = weight_grad[...] * weight[...].astype(F32)
    ones = jnp.ones((8, product.shape[1]), F32)
    total = lax.dot_general(
        ones, product, (((1,), (1,)), ((), ())),
        precision=lax.Precision.HIGHEST, preferred_element_type=F32,
    )
    return total[0:1] / gain[...].astype(F32)


def shape(dims, dtype):
    return jax.ShapeDtypeStruct(tuple(dims), dtype)


def grid_sizes(count):
    chips = count // 2
    return {16: (4, 2, 2, 2), 64: (4, 4, 4, 2)}.get(chips, (chips, 1, 1, 2))


def run_layer(sizes, counts, gains, returns, tokens, weights, frames_cot, logits_cot):
    rows, width = tokens.shape
    qkv_w, out_w, up_w, down_w, hid_w, logit_w = weights
    group = (qkv_w.shape[0], 3 * GROUP)
    blocks = [w.shape for w in (out_w, up_w, down_w, hid_w, logit_w)]
    bufs = [shape(tuple(sizes) + (16, 128), F32), shape((2,) + tuple(sizes) + group, BF16)]
    bufs += [shape(tuple(sizes) + tuple(b), BF16) for b in blocks]
    scatter_blocks = [logit_w.shape, hid_w.shape, down_w.shape, up_w.shape, out_w.shape, group, group]
    slots = [s for block in scatter_blocks for s in slot_shapes(sizes, *block)]
    peers = sum(s - 1 for s in sizes)
    vmem = pl.BlockSpec(memory_space=pltpu.VMEM)
    any_space = pl.BlockSpec(memory_space=pl.ANY)
    own = gains[0].shape[1]
    hidden = up_w.shape[1]
    return pl.pallas_call(
        functools.partial(layer_kernel, sizes),
        out_shape=[
            shape((rows, width), BF16),
            shape((rows, width), BF16),
            bufs[6],
            shape((rows, width), F32),
            shape((rows + QB, 3 * width), BF16),
            shape((rows, width), BF16),
            shape((rows, 128), F32),
            *[shape(w.shape, F32) for w in weights],
            shape((1, own), F32),
            shape((1, own), F32),
        ],
        in_specs=[pl.BlockSpec(memory_space=pltpu.SMEM)] + [vmem] * 3 + [any_space] * 9,
        out_specs=[any_space] * 7 + [vmem] * 8,
        scratch_shapes=[
            pltpu.VMEM((rows, width), BF16),
            pltpu.VMEM((rows, 128), F32),
            pltpu.VMEM((rows, width), BF16),
            pltpu.VMEM((rows, width), F32),
            pltpu.VMEM((rows, width), BF16),
            pltpu.VMEM((2, rows // QB, 4 * QB, 2 * QB), BF16),
            pltpu.VMEM((rows + QB, hidden), BF16),
            pltpu.VMEM((rows + QB, hidden), BF16),
            pltpu.VMEM((2, 4 * QB, GROUP), BF16),
            pltpu.VMEM((2, QB, GROUP), F32),
            pltpu.VMEM(up_w.shape, BF16),
            pltpu.VMEM(qkv_w.shape, BF16),
            *[pltpu.VMEM(b.shape, b.dtype) for b in bufs],
            pltpu.VMEM(bufs[1].shape, BF16),
            *[pltpu.VMEM(s, BF16) for s in slots],
            *[pltpu.SemaphoreType.DMA((2, peers))] * 34,
            pltpu.SemaphoreType.DMA((13,)),
            pltpu.SemaphoreType.DMA((4,)),
            pltpu.SemaphoreType.DMA((10,)),
            pltpu.SemaphoreType.DMA((2, 2)),
        ],
        compiler_params=pltpu.CompilerParams(
            collective_id=0, has_side_effects=True, vmem_limit_bytes=VMEM_LIMIT
        ),
    )(counts, *gains, returns, tokens, *weights, frames_cot, logits_cot)


def finish_kernel(act_hbm, weight_hbm, *refs):
    count = (len(refs) - 5) // 3
    sources, logits_hbm, targets = refs[:count], refs[count], refs[count + 1 : 2 * count + 1]
    act, weight, logits, *held = refs[2 * count + 1 : -2]
    in_sem, out_sem = refs[-2:]
    tile = act.shape[0] // 4
    jobs = []

    def load(src, dst):
        copy = pltpu.make_async_copy(src, dst, in_sem.at[len(jobs)])
        copy.start()
        jobs.append(copy)
        return copy

    first = load(weight_hbm, weight)
    moves = []
    for i in range(4):
        part = slice(i * tile, (i + 1) * tile)
        moves.append((load(act_hbm.at[part], act.at[part]), logits, logits_hbm, part))
        for src, via, dst in zip(sources[:2], held, targets):
            moves.append((load(src.at[part], via.at[part]), via, dst, part))
    for src, via, dst in zip(sources[2:], held[2:], targets[2:]):
        moves.append((load(src, via), via, dst, slice(None)))
    stores = []
    first.wait()
    for copy, via, dst, part in moves:
        copy.wait()
        if via is logits:
            logits[part] = dot(act[part], weight[...]).astype(BF16)
        store = pltpu.make_async_copy(via.at[part], dst.at[part], out_sem.at[len(stores)])
        store.start()
        stores.append(store)
    for store in stores:
        store.wait()


def run_finish(act, weight, arrays):
    logits = shape((act.shape[0], weight.shape[1]), BF16)
    any_space = pl.BlockSpec(memory_space=pl.ANY)
    outs = [logits, *[shape(a.shape, a.dtype) for a in arrays]]
    jobs = 13 + len(arrays) - 2
    return pl.pallas_call(
        finish_kernel,
        in_specs=[any_space] * (2 + len(arrays)),
        out_specs=[any_space] * len(outs),
        out_shape=outs,
        scratch_shapes=[
            *[pltpu.VMEM(a.shape, a.dtype) for a in (act, weight, *outs)],
            pltpu.SemaphoreType.DMA((jobs,)),
            pltpu.SemaphoreType.DMA((jobs,)),
        ],
        compiler_params=pltpu.CompilerParams(vmem_limit_bytes=VMEM_LIMIT),
    )(act, weight, *arrays)


def shards(
    sizes,
    tokens,
    seq_counts,
    returns,
    ln1_gain,
    qkv_weight,
    out_weight,
    ln2_gain,
    up_weight,
    down_weight,
    prior_hidden_weight,
    prior_logit_weight,
    frames_cot,
    logits_cot,
):
    own = ln1_gain.shape[0]
    (
        frames, act, w_logit, tokens_grad, _, _, _,
        o_qkv, o_out, o_up, o_down, o_hid, o_logit, o_one, o_two,
    ) = run_layer(
        sizes, seq_counts, (ln1_gain.reshape(1, own), ln2_gain.reshape(1, own)), returns.reshape(-1, 128),
        tokens, (qkv_weight, out_weight, up_weight, down_weight, prior_hidden_weight, prior_logit_weight),
        frames_cot, logits_cot,
    )
    logits, frames, tokens_grad, o_qkv, o_out, o_up, o_down, o_hid, o_logit = run_finish(
        act, w_logit.reshape(-1, w_logit.shape[-1]),
        (frames, tokens_grad, o_qkv, o_out, o_up, o_down, o_hid, o_logit),
    )
    return (
        frames, logits, tokens_grad, o_one.reshape(own), o_qkv, o_out, o_two.reshape(own),
        o_up, o_down, o_hid, o_logit,
    )


def solution(mesh):
    sizes = grid_sizes(mesh.shape["fsdp"])
    row = P("fsdp", None)
    vector = P("fsdp")
    return jax.shard_map(
        functools.partial(shards, sizes),
        mesh=mesh,
        in_specs=(row, row, vector, vector, row, row, vector, row, row, row, row, row, row),
        out_specs=(row, row, row, vector, row, row, vector, row, row, row, row),
        check_vma=False,
    )
```

```python
import functools
import math

import jax
import jax.numpy as jnp
from jax import lax
from jax.experimental import pallas as pl
from jax.experimental.pallas import tpu as pltpu
from jax.sharding import PartitionSpec as P

HEAD_DIM = 64
LONG_LEN = 64
SHORT_LEN = 50
QB = 64
BATCH = 8
GROUP = 256
F32 = jnp.float32
BF16 = jnp.bfloat16
MESH = pl.DeviceIdType.MESH
VMEM_LIMIT = 63 * 2**20


def dot(left, right):
    return jnp.dot(left, right, preferred_element_type=F32)


def dot_t(left, right):
    return lax.dot_general(left, right, (((1,), (1,)), ((), ())), preferred_element_type=F32)


def t_dot(left, right):
    return lax.dot_general(left, right, (((0,), (0,)), ((), ())), preferred_element_type=F32)


def normalize(rows):
    centred = rows - jnp.mean(rows, axis=-1, keepdims=True)
    inv_std = lax.rsqrt(jnp.mean(centred * centred, axis=-1, keepdims=True) + 1e-05)
    return centred * inv_std, inv_std


def norm_back(grad, normed, inv_std, gain):
    scaled = grad * gain
    centre = jnp.mean(scaled, axis=-1, keepdims=True)
    slope = jnp.mean(scaled * normed, axis=-1, keepdims=True)
    return inv_std * (scaled - centre - normed * slope)


def gain_row(block, first):
    return jnp.concatenate([block[first + i : first + i + 1, :] for i in range(4)], axis=1)


def loop(count, body, hooks=()):
    def one(i, carry):
        body(i)
        for turn, condition, hook in hooks:
            pl.when((i == turn - 1) & condition)(hook)
        return carry

    lax.fori_loop(0, count, one, 0)


class Place:
    def __init__(self, sizes):
        self.sizes = sizes
        self.me = lax.axis_index("fsdp")
        self.strides = [math.prod(sizes[d + 1 :]) for d in range(4)]
        self.digit = [lax.rem(self.me // self.strides[d], sizes[d]) for d in range(4)]
        self.count = math.prod(sizes)
        self.others = [
            [lax.rem(self.digit[d] + k, sizes[d]) for k in range(sizes[d])] for d in range(4)
        ]
        self.devices = [
            [self.me + (other - self.digit[d]) * self.strides[d] for other in self.others[d]]
            for d in range(4)
        ]

    def barrier(self):
        barrier = pltpu.get_barrier_semaphore()
        count = 0
        for dim in range(4):
            for k in range(1, self.sizes[dim]):
                pl.semaphore_signal(
                    barrier, inc=1, device_id=(self.devices[dim][k],), device_id_type=MESH
                )
                count += 1
        pl.semaphore_wait(barrier, count)


class Transfer:
    def __init__(self, place, order, send, recv, half):
        self.place, self.order = place, order
        self.send, self.recv, self.half = send, recv, half

    def copies(self, stage):
        place, dim = self.place, self.order[stage]
        slot = sum(place.sizes[d] - 1 for d in self.order[:stage])
        for k in range(1, place.sizes[dim]):
            src, dst = self.ends(stage, k)
            yield pltpu.make_async_remote_copy(
                src_ref=src,
                dst_ref=dst,
                send_sem=self.send.at[self.half, slot + k - 1],
                recv_sem=self.recv.at[self.half, slot + k - 1],
                device_id=(place.devices[dim][k],),
                device_id_type=MESH,
            )

    def launch(self, stage):
        for copy in self.copies(stage):
            copy.start()

    def arrive(self, stage):
        for copy in self.copies(stage):
            copy.wait_recv()

    def finish(self):
        for stage in range(4):
            for copy in self.copies(stage):
                copy.wait_send()


class GatherHalf(Transfer):
    def __init__(self, place, buf, cols, order, send, recv, half):
        super().__init__(place, tuple(order) + (3,), send, recv, half)
        self.buf, self.cols = buf, cols

    def ends(self, stage, k):
        done = self.order[:stage]
        index = tuple(slice(None) if d in done else self.place.digit[d] for d in range(4))
        block = self.buf.at[index + (slice(None), self.cols)]
        return block, block


class ScatterHalf(Transfer):
    def __init__(self, place, src, cols, slots, order, send, recv, half):
        super().__init__(place, (3,) + tuple(order[::-1]), send, recv, half)
        self.src, self.cols, self.slots = src, cols, slots

    def pick(self, stage, digit):
        left = [d for d in range(4) if d not in self.order[:stage]]
        index = tuple(digit if d == self.order[stage] else slice(None) for d in left)
        if stage == 0:
            return self.src.at[index + (slice(None), self.cols)]
        return self.slots[stage - 1].at[(0,) + index]

    def ends(self, stage, k):
        there = self.place.others[self.order[stage]][k]
        return self.pick(stage, there), self.slots[stage].at[k - 1]

    def total(self, stage, index):
        dim = self.order[stage]
        total = self.pick(stage, self.place.digit[dim])[index].astype(F32)
        for k in range(self.place.sizes[dim] - 1):
            total = total + self.slots[stage][(k,) + index].astype(F32)
        return total

    def combine(self, stage):
        self.arrive(stage)
        slots = self.slots[stage]

        def one(i):
            slots[0, i] = self.total(stage, (i,)).astype(BF16)

        loop(slots.shape[1], one)

    def result(self):
        self.arrive(3)
        return self.total(3, (Ellipsis,))


ORDERS = ((0, 2, 1), (0, 1, 2))


def halves(width, first=0):
    middle = first + width // 2
    return [slice(first, middle), slice(middle, first + width)]


class Gather:
    def __init__(self, place, buf, first, width, send, recv):
        parts = halves(width, first) if width >= 256 else [slice(0, width)]
        self.parts = [
            GatherHalf(place, buf, cols, ORDERS[h], send, recv, h) for h, cols in enumerate(parts)
        ]

    def step(self, stage):
        for part in self.parts:
            if stage:
                part.arrive(stage - 1)
            if stage < 4:
                part.launch(stage)

    def finish(self):
        for part in self.parts:
            part.finish()


class Scatter:
    def __init__(self, place, src, slots, send, recv, out):
        self.out = out
        self.cols = halves(src.shape[-1])
        self.parts = [
            ScatterHalf(place, src, self.cols[h], slots[4 * h : 4 * h + 4], ORDERS[h], send, recv, h)
            for h in range(2)
        ]

    def step(self, stage):
        for part, cols in zip(self.parts, self.cols):
            if stage == 4:
                self.out(cols, part.result())
                continue
            if stage:
                part.combine(stage - 1)
            part.launch(stage)

    def finish(self):
        for part in self.parts:
            part.finish()


def slot_shapes(sizes, rows, cols):
    shapes = []
    for order in ORDERS:
        left = [0, 1, 2, 3]
        for dim in (3,) + tuple(order[::-1]):
            left.remove(dim)
            shapes.append((sizes[dim] - 1,) + tuple(sizes[d] for d in left) + (rows, cols // 2))
    return shapes


def head_masks(value):
    row = lax.broadcasted_iota(jnp.int32, (4 * QB, GROUP), 0) // QB
    col = lax.broadcasted_iota(jnp.int32, (4 * QB, GROUP), 1) // HEAD_DIM
    return jnp.where(row == col, value, 0.0).astype(BF16)


def stack_heads(block, mask):
    return jnp.concatenate([block] * 4, axis=0) * mask


def pick_heads(stacked):
    col = lax.broadcasted_iota(jnp.int32, (QB, GROUP), 1) // HEAD_DIM
    parts = [stacked[h * QB : (h + 1) * QB] for h in range(4)]
    return jnp.where(
        col < 2,
        jnp.where(col == 0, parts[0], parts[1]),
        jnp.where(col == 2, parts[2], parts[3]),
    )


def score_bias(step, long_end, short_end):
    row = step * QB + lax.broadcasted_iota(jnp.int32, (QB, 2 * QB), 0)
    key = (step - 1) * QB + lax.broadcasted_iota(jnp.int32, (QB, 2 * QB), 1)
    past = (row - long_end).astype(F32)
    number = jnp.floor((past + 0.5) * (1.0 / SHORT_LEN)).astype(jnp.int32)
    begin = jnp.where(
        row < long_end,
        step * QB,
        jnp.where(row < short_end, long_end + number * SHORT_LEN, row),
    )
    return jnp.where((key >= begin) & (key <= row), 0.0, -1e30)


def row_block(step, count=1):
    return pl.ds(pl.multiple_of(step * QB, QB), count * QB)


def columns(i, size, offset=0):
    return pl.ds(pl.multiple_of(offset + i * size, 128), size)


def group_columns(g):
    return [columns(3 * g + part, GROUP) for part in range(3)]


def attend_steps(g, first, count, qkv_ref, probs_ref, att_ref, mask, long_end, short_end):
    query_cols, key_cols, value_cols = group_columns(g)
    work = []
    for step in [first + u for u in range(count)]:
        bias = score_bias(step, long_end, short_end)
        bias = jnp.concatenate([bias] * 4, axis=0)
        query = stack_heads(qkv_ref[row_block(step + 1), query_cols], mask)
        keys = qkv_ref[row_block(step, 2), key_cols]
        work.append((step, dot_t(query, keys) + bias))
    done = []
    for step, scores in work:
        weight = jnp.exp(scores - jnp.max(scores, axis=-1, keepdims=True))
        total = jnp.sum(weight, axis=-1, keepdims=True)
        probs = (weight * pl.reciprocal(total)).astype(BF16)
        probs_ref[g, step] = probs
        done.append((step, probs))
    for step, probs in done:
        values = qkv_ref[row_block(step, 2), value_cols]
        mixed = pick_heads(dot(probs, values))
        att_ref[row_block(step), columns(g, GROUP)] = mixed.astype(BF16)


def attend_back_steps(g, first, count, qkv_ref, probs_ref, grad_ref, back_ref, carry_ref, masks_ref):
    query_cols, key_cols, value_cols = group_columns(g)
    mask, scaled_mask = masks_ref[0], masks_ref[1]
    work = []
    for step in [first + u for u in range(count)]:
        query = stack_heads(qkv_ref[row_block(step + 1), query_cols], scaled_mask)
        keys = qkv_ref[row_block(step, 2), key_cols]
        values = qkv_ref[row_block(step, 2), value_cols]
        grad = stack_heads(grad_ref[row_block(step), columns(g, GROUP)], mask)
        work.append((step, query, keys, grad, dot_t(grad, values)))
    score_grads = []
    for step, _, _, _, prob_grad in work:
        probs = probs_ref[g, step].astype(F32)
        product = probs * prob_grad
        inner = jnp.sum(product, axis=-1, keepdims=True)
        score_grads.append((product - probs * inner).astype(BF16))
    held = [carry_ref[0], carry_ref[1]]
    for (step, query, keys, grad, _), score_grad in zip(work, score_grads):
        query_grad = pick_heads(dot(score_grad, keys)) * HEAD_DIM ** (-0.5)
        back_ref[row_block(step + 1), query_cols] = query_grad.astype(BF16)
        both = (t_dot(score_grad, query), t_dot(probs_ref[g, step], grad))
        for part, (cols, grads) in enumerate(zip((key_cols, value_cols), both)):
            back_ref[row_block(step), cols] = (held[part] + grads[:QB]).astype(BF16)
            held[part] = grads[QB:]
    for part in range(2):
        carry_ref[part] = held[part]


GATHER_PLAN = {
    "start": {0: ("aux0", "a0", "b0", "aux1", "out0", "a1", "up00", "aux2", "b1", "up10", "aux3", "a2", "out1", "aux4")},
    "norm": {1: ("down00", "b2"), 2: ("up01", "a3")},
    "qkv_a": {0: ("down10", "out2", "up11", "a4"), 2: ("b3", "hid0")},
    "attend_a": {1: ("up02", "down01"), 2: ("logit0",), 3: ("out3",), 4: ("down11",)},
    "qkv_b": {0: ("b4",), 1: ("up12",), 2: ("hid1",)},
    "attend_b": {1: ("up03",), 3: ("down02", "logit1")},
    "out": {0: ("out4",), 1: ("down12",)},
    "up": {0: ("up04",), 1: ("up13",), 2: ("up14", "hid2"), 3: ("down03",), 4: ("logit2",)},
    "down": {0: ("down04",), 1: ("down13",), 2: ("down14", "hid3"), 4: ("logit3",)},
    "head": {0: ("hid4", "logit4")},
}
SCATTER_PLAN = {
    "sums": {0: ("logit0", "hid0")},
    "up_back": {1: ("logit1", "hid1")},
    "down_grad": {2: ("logit2", "hid2", "down0")},
    "norm_back": {1: ("logit3", "hid3", "down1")},
    "up_grad": {2: ("down2", "up0")},
    "out_back": {1: ("logit4", "hid4"), 2: ("up1",)},
    "out_grad": {0: ("out0",)},
    "back_a": {1: ("out1", "down3")},
    "grad_a": {0: ("a0",)},
    "back_b": {1: ("up2",), 2: ("a1", "out2"), 4: ("down4",)},
    "grad_b": {0: ("up3", "b0")},
    "token": {1: ("b1", "a2", "out3")},
    "end": {0: ("b2", "a3", "out4", "up4", "b3", "a4", "b4")},
}


def layer_kernel(sizes, *refs):
    (
        counts, gain_one_in, gain_two_in, returns_in,
        tokens_hbm, qkv_in, out_in, up_in, down_in, hid_in, logit_in, frames_cot, logits_cot,
        frames_hbm, act_hbm, logit_hbm, grad_hbm, qkv_hbm, norm_hbm, inv_hbm,
        o_qkv, o_out, o_up, o_down, o_hid, o_logit, o_one, o_two,
        norm_ref, inv_ref, att_ref, back_ref, frames_ref, probs_ref, wide_a, wide_b,
        masks_ref, carry_ref, own_up, own_qkv,
        *rest,
    ) = refs
    bufs, rest = rest[:7], rest[7:]
    g_qkv, rest = rest[0], rest[1:]
    slots, rest = [rest[8 * i : 8 * i + 8] for i in range(7)], rest[56:]
    g_sems, rest = [rest[2 * i : 2 * i + 2] for i in range(10)], rest[20:]
    s_sems, rest = [rest[2 * i : 2 * i + 2] for i in range(7)], rest[14:]
    own_sem, in_sem, out_sem, cot_sem = rest
    aux_buf, qkv_buf, out_buf, up_buf, down_buf, hid_buf, logit_buf = bufs

    place = Place(sizes)
    rows, width = back_ref.shape
    hidden = up_buf.shape[-1]
    three = 3 * width
    tile = 512
    tall = 1024
    long_end = counts[0, 0] * LONG_LEN
    short_end = long_end + counts[0, 1] * SHORT_LEN

    def at(i, size=tile, offset=0):
        return pl.ds(pl.multiple_of(offset + i * size, QB), size)

    def start(src, dst, sem):
        copy = pltpu.make_async_copy(src, dst, sem)
        copy.start()
        return copy

    def whole(buf):
        return buf[...].reshape(-1, buf.shape[-1])

    def put(ref):
        def store_out(cols, value):
            ref[:, cols] = value

        return store_out

    def put_group(g):
        def store_out(cols, value):
            first = cols.start
            while first < cols.stop:
                last = min(cols.stop, (first // GROUP + 1) * GROUP)
                to = first // GROUP * 2 * GROUP + GROUP * g + first % GROUP
                o_qkv[:, to : to + last - first] = value[:, first - cols.start : last - cols.start]
                first = last

        return store_out

    def buffers(*pairs):
        return {
            name: Gather(place, buf, first, cols, *g_sems[i])
            for i, (name, buf, first, cols) in enumerate(pairs)
        }

    gathers = buffers(
        ("aux", aux_buf, 0, 128),
        ("a", qkv_buf.at[0], 0, 3 * GROUP),
        ("b", qkv_buf.at[1], 0, 3 * GROUP),
        ("out", out_buf, 0, width),
        ("up0", up_buf, 0, hidden // 2),
        ("up1", up_buf, hidden // 2, hidden // 2),
        ("down0", down_buf, 0, width // 2),
        ("down1", down_buf, width // 2, width // 2),
        ("hid", hid_buf, 0, hid_buf.shape[-1]),
        ("logit", logit_buf, 0, logit_buf.shape[-1]),
    )
    scatters = {
        name: Scatter(place, src, slots[i], *s_sems[i], out)
        for i, (name, src, out) in enumerate((
            ("logit", logit_buf, put(o_logit)),
            ("hid", hid_buf, put(o_hid)),
            ("down", down_buf, put(o_down)),
            ("up", up_buf, put(o_up)),
            ("out", out_buf, put(o_out)),
            ("a", g_qkv.at[0], put_group(0)),
            ("b", g_qkv.at[1], put_group(1)),
        ))
    }

    def transfers(*phases, group=0):
        hooks = []
        for g, phase in enumerate(phases):
            turns = {}
            for plan, items in ((GATHER_PLAN, gathers), (SCATTER_PLAN, scatters)):
                for turn, steps in plan.get(phase, {}).items():
                    turns.setdefault(turn, []).extend((items[s[:-1]], int(s[-1])) for s in steps)

            def run(steps):
                for item, stage in steps:
                    item.step(stage)

            for turn, steps in turns.items():
                hook = functools.partial(run, steps)
                if turn:
                    hooks.append((turn, True if len(phases) == 1 else group == g, hook))
                elif len(phases) == 1:
                    hook()
                else:
                    pl.when(group == g)(hook)
        return hooks

    own = []
    for g in range(2):
        for part in range(3):
            first = 2 * GROUP * part + GROUP * g
            target = qkv_buf.at[(g, *place.digit, slice(None), slice(GROUP * part, GROUP * (part + 1)))]
            own.append(start(qkv_in.at[:, first : first + GROUP], target, own_sem.at[len(own)]))
    for src, buf in ((out_in, out_buf), (up_in, up_buf), (down_in, down_buf), (hid_in, hid_buf), (logit_in, logit_buf)):
        own.append(start(src, buf.at[tuple(place.digit)], own_sem.at[len(own)]))
    own.append(start(up_in, own_up, own_sem.at[11]))
    own.append(start(qkv_in, own_qkv, own_sem.at[12]))
    aux_buf[tuple(place.digit)] = own_block(place, gain_one_in, gain_two_in, returns_in)
    masks_ref[0] = head_masks(1.0)
    masks_ref[1] = head_masks(HEAD_DIM ** (-0.5))
    place.barrier()
    for copy in own:
        copy.wait()

    def gains():
        aux = jnp.sum(aux_buf[...].reshape(-1, *aux_buf.shape[-2:]), axis=0)
        return gain_row(aux, 0), gain_row(aux, 4), place.count / aux[8:9, 0:1]

    def norm_gradient(i, size, grad, gain):
        normed = norm_ref[at(i, size), :].astype(F32) * (1.0 / gain)
        back_ref[at(i, size), :] += norm_back(grad, normed, inv_ref[at(i, size), 0:1], gain)

    def forward(tokens):
        tokens_copy = start(tokens_hbm, tokens, in_sem.at[0])
        transfers("start")
        gain_one, gain_two, _ = gains()
        tokens_copy.wait()

        def norm_tile(i):
            normed, inv_std = normalize(tokens[at(i, tall), :].astype(F32))
            norm_ref[at(i, tall), :] = (normed * gain_one).astype(BF16)
            inv_ref[at(i, tall), :] = jnp.broadcast_to(inv_std, (tall, inv_ref.shape[1]))

        loop(rows // tall, norm_tile, transfers("norm"))
        start(norm_ref, norm_hbm, out_sem.at[6])
        start(inv_ref, inv_hbm, out_sem.at[7])
        wide_a[0:QB, 0:three] = jnp.zeros((QB, three), BF16)

        def group(g):
            hooks = transfers("qkv_a", "qkv_b", group=g)
            cols = columns(g, 3 * GROUP)

            def qkv_tile(i):
                weight = qkv_buf[g].reshape(width, -1)
                wide_a[at(i, tall, QB), cols] = dot(norm_ref[at(i, tall), :], weight).astype(BF16)

            loop(rows // tall, qkv_tile, hooks)

            @pl.when(g == 1)
            def _():
                start(wide_a.at[:, 0:three], qkv_hbm, out_sem.at[0])

            def attend(i):
                attend_steps(g, i * BATCH, BATCH, wide_a, probs_ref, att_ref, masks_ref[1], long_end, short_end)

            loop(rows // QB // BATCH, attend, transfers("attend_a", "attend_b", group=g))

        loop(2, group)
        pltpu.make_async_copy(norm_ref, norm_hbm, out_sem.at[6]).wait()
        pltpu.make_async_copy(inv_ref, inv_hbm, out_sem.at[7]).wait()
        hooks = transfers("out")

        def out_tile(i):
            residual = tokens[at(i), :].astype(F32) + dot(att_ref[at(i), :], whole(out_buf))
            back_ref[at(i), :] = residual
            normed, inv_std = normalize(residual)
            norm_ref[at(i), :] = (normed * gain_two).astype(BF16)
            inv_ref[at(i), :] = jnp.broadcast_to(inv_std, (tile, inv_ref.shape[1]))

        loop(rows // tile, out_tile, hooks)

    pl.run_scoped(forward, pltpu.VMEM((rows, width), BF16))
    pltpu.make_async_copy(wide_a.at[:, 0:three], qkv_hbm, out_sem.at[0]).wait()

    def feed_forward(fcot, lcot, ha_ref, sum_logit, sum_hid):
        _, gain_two, inverse_scale = gains()

        def cotangents(i, slot):
            return [
                pltpu.make_async_copy(frames_cot.at[at(i), :], fcot.at[slot], cot_sem.at[0, slot]),
                pltpu.make_async_copy(logits_cot.at[at(i), :], lcot.at[slot], cot_sem.at[1, slot]),
            ]

        for copy in cotangents(0, 0):
            copy.start()
        hooks = transfers("up")

        def up_tile(i):
            rows_at = at(lax.rem(i, 2), tall)
            for part in range(2):
                cols = columns(2 * (i // 2) + part, hidden // 4)
                value = dot(norm_ref[rows_at, :], up_buf[..., cols].reshape(width, -1))
                slope = jnp.exp(jnp.minimum(value, 0.0))
                wide_b[rows_at, cols] = slope.astype(BF16)
                wide_a[rows_at, cols] = jnp.where(value > 0, value, slope - 1.0).astype(BF16)

        loop(2 * rows // tall, up_tile, hooks)
        hooks = transfers("down")

        def down_tile(i):
            rows_at = at(lax.rem(i, 2), tall)
            cols = columns(i // 2, width // 2)
            value = dot(wide_a[rows_at, 0:hidden], down_buf[..., cols].reshape(hidden, -1))
            frames_ref[rows_at, cols] = (back_ref[rows_at, cols] + value).astype(BF16)

        loop(2 * rows // tall, down_tile, hooks)
        frames_copy = start(frames_ref, frames_hbm, out_sem.at[1])
        transfers("head")
        logit_copy = start(logit_buf, logit_hbm, out_sem.at[8])
        for item in gathers.values():
            item.finish()
        sum_logit[...] = jnp.zeros_like(sum_logit)
        sum_hid[...] = jnp.zeros_like(sum_hid)
        frames_copy.wait()

        def head_tile(i):
            slot = lax.rem(i, 2)

            @pl.when(i + 1 < rows // tile)
            def _():
                for copy in cotangents(i + 1, lax.rem(i + 1, 2)):
                    copy.start()

            for copy in cotangents(i, slot):
                copy.wait()
            row = i * tile + lax.broadcasted_iota(jnp.int32, (tile, 1), 0)
            live = jnp.where(row < short_end, 1.0, 0.0)
            logit_back = (lcot[slot].astype(F32) * (live * inverse_scale)).astype(BF16)
            head_in = frames_ref[at(i), :]
            hidden_rows = dot(head_in, whole(hid_buf))
            act_back = dot_t(logit_back, whole(logit_buf))
            slope = jnp.exp(jnp.minimum(hidden_rows, 0.0))
            hidden_act = jnp.where(hidden_rows > 0, hidden_rows, slope - 1.0).astype(BF16)
            hidden_back = (act_back * slope).astype(BF16)
            ha_ref[at(i), :] = hidden_act
            sum_logit[...] += t_dot(hidden_act, logit_back)
            stream_back = fcot[slot].astype(F32) * live + dot_t(hidden_back, whole(hid_buf))
            sum_hid[...] += t_dot(head_in, hidden_back)
            back_ref[at(i), :] = stream_back
            frames_ref[at(i), :] = stream_back.astype(BF16)

        loop(rows // tile, head_tile)
        act_copy = start(ha_ref, act_hbm, out_sem.at[9])
        logit_copy.wait()
        logit_buf[...] = sum_logit[...].astype(BF16).reshape(logit_buf.shape)
        hid_buf[...] = sum_hid[...].astype(BF16).reshape(hid_buf.shape)
        transfers("sums")

        def up_back_tile(i):
            for part in range(4):
                cols = slice(part * hidden // 4, (part + 1) * hidden // 4)
                grad = dot_t(frames_ref[at(i, tall), :], whole(down_buf)[cols])
                slope = wide_b[at(i, tall), cols].astype(F32)
                wide_b[at(i, tall), cols] = (grad * slope).astype(BF16)

        loop(rows // tall, up_back_tile, transfers("up_back"))
        act_copy.wait()


        def down_grad(i):
            count = sizes[0] // 2
            grad = t_dot(wide_a[0:rows, columns(i, hidden // 2)], frames_ref[...])
            down_buf[pl.ds(i * count, count)] = grad.astype(BF16).reshape((count,) + down_buf.shape[1:])

        loop(2, down_grad, transfers("down_grad"))
        start(qkv_hbm, wide_a.at[:, 0:three], in_sem.at[1])

        def norm_back_tile(i):
            grad = dot_t(wide_b[at(i, tall), 0:hidden], whole(up_buf))
            norm_gradient(i, tall, grad, gain_two)

        loop(rows // tall, norm_back_tile, transfers("norm_back"))

        def up_grad(i):
            cols = columns(i, hidden // 2)
            grad = t_dot(norm_ref[...], wide_b[0:rows, cols])
            up_buf[..., cols] = grad.astype(BF16).reshape(up_buf.shape[:-1] + (-1,))

        loop(2, up_grad, transfers("up_grad"))
        start(norm_hbm, norm_ref, in_sem.at[2])
        start(inv_hbm, inv_ref, in_sem.at[3])

    pl.run_scoped(
        feed_forward,
        pltpu.VMEM((2, tile, frames_cot.shape[1]), BF16),
        pltpu.VMEM((2, tile, logits_cot.shape[1]), BF16),
        pltpu.VMEM((rows, width), BF16),
        pltpu.VMEM((width, logits_cot.shape[1]), F32),
        pltpu.VMEM((width, width), F32),
    )

    gain_one, _, _ = gains()

    def out_back_tile(i):
        out_back = back_ref[at(i, tall), :].astype(BF16)
        frames_ref[at(i, tall), :] = dot_t(out_back, whole(out_buf)).astype(BF16)

    loop(rows // tall, out_back_tile, transfers("out_back"))
    grad = t_dot(att_ref[...], back_ref[...].astype(BF16))
    out_buf[...] = grad.astype(BF16).reshape(out_buf.shape)
    transfers("out_grad")
    pltpu.make_async_copy(qkv_hbm, wide_a.at[:, 0:three], in_sem.at[1]).wait()
    pltpu.make_async_copy(norm_hbm, norm_ref, in_sem.at[2]).wait()
    pltpu.make_async_copy(inv_hbm, inv_ref, in_sem.at[3]).wait()

    def group_back(g):
        carry_ref[...] = jnp.zeros_like(carry_ref)

        def attend_back(i):
            attend_back_steps(g, i * BATCH, BATCH, wide_a, probs_ref, frames_ref, wide_b, carry_ref, masks_ref)

        loop(rows // QB // BATCH, attend_back, transfers("back_a", "back_b", group=g))
        for part, cols in enumerate(group_columns(g)[1:]):
            wide_b[rows : rows + QB, cols] = carry_ref[part].astype(BF16)
        grad = t_dot(norm_ref[...], wide_b[QB : QB + rows, columns(g, 3 * GROUP)])
        g_qkv[g] = grad.astype(BF16).reshape(g_qkv.shape[1:])
        transfers("grad_a", "grad_b", group=g)

    loop(2, group_back)
    hooks = transfers("token")

    def token_tile(i):
        grad = dot_t(wide_b[at(i, offset=QB), 0 : 3 * GROUP], qkv_buf[0].reshape(width, -1))
        grad += dot_t(wide_b[at(i, offset=QB), 3 * GROUP : three], qkv_buf[1].reshape(width, -1))
        norm_gradient(i, tile, grad, gain_one)
        frames_ref[at(i), :] = back_ref[at(i), :].astype(BF16)
        start(frames_ref.at[at(i), :], grad_hbm.at[at(i), :], out_sem.at[2 + i])

    loop(rows // tile, token_tile, hooks)
    transfers("end")
    o_two[...] = gain_grad(o_up, own_up, gain_two_in)
    o_one[...] = gain_grad(o_qkv, own_qkv, gain_one_in)
    for item in scatters.values():
        item.finish()
    for i in range(rows // tile):
        pltpu.make_async_copy(frames_ref.at[at(i), :], grad_hbm.at[at(i), :], out_sem.at[2 + i]).wait()


def own_block(place, gain_one, gain_two, returns):
    own = gain_one.shape[1]
    row = lax.broadcasted_iota(jnp.int32, (4, 128), 0)
    lane = lax.broadcasted_iota(jnp.int32, (4, 128), 1)
    mine = (row * 128 + lane) // own == place.me
    pick_row = lax.broadcasted_iota(jnp.int32, (own, 128), 0)
    pick_lane = lax.broadcasted_iota(jnp.int32, (own, 128), 1)
    pick = jnp.where(lax.rem(pick_lane, own) == pick_row, 1.0, 0.0).astype(BF16)
    spread = [
        jnp.where(mine, jnp.broadcast_to(dot(gain[...], pick), (4, 128)), 0.0)
        for gain in (gain_one, gain_two)
    ]
    time = lax.broadcasted_iota(jnp.int32, returns.shape, 0) * returns.shape[1]
    time = time + lax.broadcasted_iota(jnp.int32, returns.shape, 1)
    steps_back = (returns.shape[0] * returns.shape[1] - 1 - time).astype(F32)
    decays = 0.01 * jnp.exp(steps_back * math.log(0.99))
    terms = jnp.sum(returns[...].astype(F32) * decays, axis=0, keepdims=True)
    mean = jnp.sum(terms, axis=1, keepdims=True)
    return jnp.concatenate(spread + [jnp.broadcast_to(mean, (8, 128))], axis=0)


def gain_grad(weight_grad, weight, gain):
    product = weight_grad[...] * weight[...].astype(F32)
    ones = jnp.ones((8, product.shape[1]), F32)
    total = lax.dot_general(
        ones, product, (((1,), (1,)), ((), ())),
        precision=lax.Precision.HIGHEST, preferred_element_type=F32,
    )
    return total[0:1] / gain[...].astype(F32)


def shape(dims, dtype):
    return jax.ShapeDtypeStruct(tuple(dims), dtype)


def grid_sizes(count):
    chips = count // 2
    return {16: (4, 2, 2, 2), 64: (4, 4, 4, 2)}.get(chips, (chips, 1, 1, 2))


def run_layer(sizes, counts, gains, returns, tokens, weights, frames_cot, logits_cot):
    rows, width = tokens.shape
    qkv_w, out_w, up_w, down_w, hid_w, logit_w = weights
    group = (qkv_w.shape[0], 3 * GROUP)
    blocks = [w.shape for w in (out_w, up_w, down_w, hid_w, logit_w)]
    bufs = [shape(tuple(sizes) + (16, 128), F32), shape((2,) + tuple(sizes) + group, BF16)]
    bufs += [shape(tuple(sizes) + tuple(b), BF16) for b in blocks]
    scatter_blocks = [logit_w.shape, hid_w.shape, down_w.shape, up_w.shape, out_w.shape, group, group]
    slots = [s for block in scatter_blocks for s in slot_shapes(sizes, *block)]
    peers = sum(s - 1 for s in sizes)
    vmem = pl.BlockSpec(memory_space=pltpu.VMEM)
    any_space = pl.BlockSpec(memory_space=pl.ANY)
    own = gains[0].shape[1]
    hidden = up_w.shape[1]
    return pl.pallas_call(
        functools.partial(layer_kernel, sizes),
        out_shape=[
            shape((rows, width), BF16),
            shape((rows, width), BF16),
            bufs[6],
            shape((rows, width), BF16),
            shape((rows + QB, 3 * width), BF16),
            shape((rows, width), BF16),
            shape((rows, 128), F32),
            *[shape(w.shape, F32) for w in weights],
            shape((1, own), F32),
            shape((1, own), F32),
        ],
        in_specs=[pl.BlockSpec(memory_space=pltpu.SMEM)] + [vmem] * 3 + [any_space] * 9,
        out_specs=[any_space] * 7 + [vmem] * 8,
        scratch_shapes=[
            pltpu.VMEM((rows, width), BF16),
            pltpu.VMEM((rows, 128), F32),
            pltpu.VMEM((rows, width), BF16),
            pltpu.VMEM((rows, width), F32),
            pltpu.VMEM((rows, width), BF16),
            pltpu.VMEM((2, rows // QB, 4 * QB, 2 * QB), BF16),
            pltpu.VMEM((rows + QB, hidden), BF16),
            pltpu.VMEM((rows + QB, hidden), BF16),
            pltpu.VMEM((2, 4 * QB, GROUP), BF16),
            pltpu.VMEM((2, QB, GROUP), F32),
            pltpu.VMEM(up_w.shape, BF16),
            pltpu.VMEM(qkv_w.shape, BF16),
            *[pltpu.VMEM(b.shape, b.dtype) for b in bufs],
            pltpu.VMEM(bufs[1].shape, BF16),
            *[pltpu.VMEM(s, BF16) for s in slots],
            *[pltpu.SemaphoreType.DMA((2, peers))] * 34,
            pltpu.SemaphoreType.DMA((13,)),
            pltpu.SemaphoreType.DMA((4,)),
            pltpu.SemaphoreType.DMA((10,)),
            pltpu.SemaphoreType.DMA((2, 2)),
        ],
        compiler_params=pltpu.CompilerParams(
            collective_id=0, has_side_effects=True, vmem_limit_bytes=VMEM_LIMIT
        ),
    )(counts, *gains, returns, tokens, *weights, frames_cot, logits_cot)


def finish_kernel(act_hbm, weight_hbm, *refs):
    count = (len(refs) - 5) // 3
    sources, logits_hbm, targets = refs[:count], refs[count], refs[count + 1 : 2 * count + 1]
    act, weight, wide, logits, *held = refs[2 * count + 1 : -2]
    in_sem, out_sem = refs[-2:]
    tile = act.shape[0] // 4
    jobs = []

    def load(src, dst):
        copy = pltpu.make_async_copy(src, dst, in_sem.at[len(jobs)])
        copy.start()
        jobs.append(copy)
        return copy

    first = load(weight_hbm, weight)
    moves = []
    for i in range(4):
        part = slice(i * tile, (i + 1) * tile)
        moves.append((load(act_hbm.at[part], act.at[part]), logits, logits_hbm, part))
        for src, via, dst in zip(sources[:2], held, targets):
            moves.append((load(src.at[part], via.at[part]), via, dst, part))
    for src, via, dst in zip(sources[2:], held[2:], targets[2:]):
        moves.append((load(src, via), via, dst, slice(None)))
    stores = []
    first.wait()
    for copy, via, dst, part in moves:
        copy.wait()
        if via is logits:
            logits[part] = dot(act[part], weight[...]).astype(BF16)
        if via is held[1]:
            wide[part] = via[part].astype(F32)
            via = wide
        store = pltpu.make_async_copy(via.at[part], dst.at[part], out_sem.at[len(stores)])
        store.start()
        stores.append(store)
    for store in stores:
        store.wait()


def run_finish(act, weight, arrays):
    logits = shape((act.shape[0], weight.shape[1]), BF16)
    any_space = pl.BlockSpec(memory_space=pl.ANY)
    wide = shape(arrays[1].shape, F32)
    outs = [logits, arrays[0], wide, *arrays[2:]]
    held = [logits, *arrays]
    jobs = 13 + len(arrays) - 2
    return pl.pallas_call(
        finish_kernel,
        in_specs=[any_space] * (2 + len(arrays)),
        out_specs=[any_space] * len(outs),
        out_shape=[shape(a.shape, a.dtype) for a in outs],
        scratch_shapes=[
            *[pltpu.VMEM(a.shape, a.dtype) for a in (act, weight, wide, *held)],
            pltpu.SemaphoreType.DMA((jobs,)),
            pltpu.SemaphoreType.DMA((jobs,)),
        ],
        compiler_params=pltpu.CompilerParams(vmem_limit_bytes=VMEM_LIMIT),
    )(act, weight, *arrays)


def shards(
    sizes,
    tokens,
    seq_counts,
    returns,
    ln1_gain,
    qkv_weight,
    out_weight,
    ln2_gain,
    up_weight,
    down_weight,
    prior_hidden_weight,
    prior_logit_weight,
    frames_cot,
    logits_cot,
):
    own = ln1_gain.shape[0]
    (
        frames, act, w_logit, tokens_grad, _, _, _,
        o_qkv, o_out, o_up, o_down, o_hid, o_logit, o_one, o_two,
    ) = run_layer(
        sizes, seq_counts, (ln1_gain.reshape(1, own), ln2_gain.reshape(1, own)), returns.reshape(-1, 128),
        tokens, (qkv_weight, out_weight, up_weight, down_weight, prior_hidden_weight, prior_logit_weight),
        frames_cot, logits_cot,
    )
    logits, frames, tokens_grad, o_qkv, o_out, o_up, o_down, o_hid, o_logit = run_finish(
        act, w_logit.reshape(-1, w_logit.shape[-1]),
        (frames, tokens_grad, o_qkv, o_out, o_up, o_down, o_hid, o_logit),
    )
    return (
        frames, logits, tokens_grad, o_one.reshape(own), o_qkv, o_out, o_two.reshape(own),
        o_up, o_down, o_hid, o_logit,
    )


def solution(mesh):
    sizes = grid_sizes(mesh.shape["fsdp"])
    row = P("fsdp", None)
    vector = P("fsdp")
    return jax.shard_map(
        functools.partial(shards, sizes),
        mesh=mesh,
        in_specs=(row, row, vector, vector, row, row, vector, row, row, row, row, row, row),
        out_specs=(row, row, row, vector, row, row, vector, row, row, row, row),
        check_vma=False,
    )
```

```python
import functools
import math

import jax
import jax.numpy as jnp
from jax import lax
from jax.experimental import pallas as pl
from jax.experimental.pallas import tpu as pltpu
from jax.sharding import PartitionSpec as P

HEAD_DIM = 64
LONG_LEN = 64
SHORT_LEN = 50
QB = 64
BATCH = 8
GROUP = 256
F32 = jnp.float32
BF16 = jnp.bfloat16
MESH = pl.DeviceIdType.MESH
VMEM_LIMIT = 63 * 2**20


def dot(left, right):
    return jnp.dot(left, right, preferred_element_type=F32)


def dot_t(left, right):
    return lax.dot_general(left, right, (((1,), (1,)), ((), ())), preferred_element_type=F32)


def t_dot(left, right):
    return lax.dot_general(left, right, (((0,), (0,)), ((), ())), preferred_element_type=F32)


def normalize(rows):
    centred = rows - jnp.mean(rows, axis=-1, keepdims=True)
    inv_std = lax.rsqrt(jnp.mean(centred * centred, axis=-1, keepdims=True) + 1e-05)
    return centred * inv_std, inv_std


def norm_back(grad, normed, inv_std, gain):
    scaled = grad * gain
    centre = jnp.mean(scaled, axis=-1, keepdims=True)
    slope = jnp.mean(scaled * normed, axis=-1, keepdims=True)
    return inv_std * (scaled - centre - normed * slope)


def gain_row(block, first):
    return jnp.concatenate([block[first + i : first + i + 1, :] for i in range(4)], axis=1)


def loop(count, body, hooks=()):
    def one(i, carry):
        body(i)
        for turn, condition, hook in hooks:
            pl.when((i == turn - 1) & condition)(hook)
        return carry

    lax.fori_loop(0, count, one, 0)


class Place:
    def __init__(self, sizes):
        self.sizes = sizes
        self.me = lax.axis_index("fsdp")
        self.strides = [math.prod(sizes[d + 1 :]) for d in range(4)]
        self.digit = [lax.rem(self.me // self.strides[d], sizes[d]) for d in range(4)]
        self.count = math.prod(sizes)
        self.others = [
            [lax.rem(self.digit[d] + k, sizes[d]) for k in range(sizes[d])] for d in range(4)
        ]
        self.devices = [
            [self.me + (other - self.digit[d]) * self.strides[d] for other in self.others[d]]
            for d in range(4)
        ]

    def barrier(self):
        barrier = pltpu.get_barrier_semaphore()
        count = 0
        for dim in range(4):
            for k in range(1, self.sizes[dim]):
                pl.semaphore_signal(
                    barrier, inc=1, device_id=(self.devices[dim][k],), device_id_type=MESH
                )
                count += 1
        pl.semaphore_wait(barrier, count)


class Transfer:
    def __init__(self, place, order, send, recv, half):
        self.place, self.order = place, order
        self.send, self.recv, self.half = send, recv, half

    def copies(self, stage):
        place, dim = self.place, self.order[stage]
        slot = sum(place.sizes[d] - 1 for d in self.order[:stage])
        for k in range(1, place.sizes[dim]):
            src, dst = self.ends(stage, k)
            yield pltpu.make_async_remote_copy(
                src_ref=src,
                dst_ref=dst,
                send_sem=self.send.at[self.half, slot + k - 1],
                recv_sem=self.recv.at[self.half, slot + k - 1],
                device_id=(place.devices[dim][k],),
                device_id_type=MESH,
            )

    def launch(self, stage):
        for copy in self.copies(stage):
            copy.start()

    def arrive(self, stage):
        for copy in self.copies(stage):
            copy.wait_recv()

    def finish(self):
        for stage in range(4):
            for copy in self.copies(stage):
                copy.wait_send()


class GatherHalf(Transfer):
    def __init__(self, place, buf, cols, order, send, recv, half):
        super().__init__(place, tuple(order) + (3,), send, recv, half)
        self.buf, self.cols = buf, cols

    def ends(self, stage, k):
        done = self.order[:stage]
        index = tuple(slice(None) if d in done else self.place.digit[d] for d in range(4))
        block = self.buf.at[index + (slice(None), self.cols)]
        return block, block


class ScatterHalf(Transfer):
    def __init__(self, place, src, cols, slots, order, send, recv, half):
        super().__init__(place, (3,) + tuple(order[::-1]), send, recv, half)
        self.src, self.cols, self.slots = src, cols, slots

    def pick(self, stage, digit):
        left = [d for d in range(4) if d not in self.order[:stage]]
        index = tuple(digit if d == self.order[stage] else slice(None) for d in left)
        if stage == 0:
            return self.src.at[index + (slice(None), self.cols)]
        return self.slots[stage - 1].at[(0,) + index]

    def ends(self, stage, k):
        there = self.place.others[self.order[stage]][k]
        return self.pick(stage, there), self.slots[stage].at[k - 1]

    def total(self, stage, index):
        dim = self.order[stage]
        total = self.pick(stage, self.place.digit[dim])[index].astype(F32)
        for k in range(self.place.sizes[dim] - 1):
            total = total + self.slots[stage][(k,) + index].astype(F32)
        return total

    def combine(self, stage):
        self.arrive(stage)
        slots = self.slots[stage]

        def one(i):
            slots[0, i] = self.total(stage, (i,)).astype(BF16)

        loop(slots.shape[1], one)

    def result(self):
        self.arrive(3)
        return self.total(3, (Ellipsis,))


ORDERS = ((0, 2, 1), (0, 1, 2))


def halves(width, first=0):
    middle = first + width // 2
    return [slice(first, middle), slice(middle, first + width)]


class Gather:
    def __init__(self, place, buf, first, width, send, recv):
        parts = halves(width, first) if width >= 256 else [slice(0, width)]
        self.parts = [
            GatherHalf(place, buf, cols, ORDERS[h], send, recv, h) for h, cols in enumerate(parts)
        ]

    def step(self, stage):
        for part in self.parts:
            if stage:
                part.arrive(stage - 1)
            if stage < 4:
                part.launch(stage)

    def finish(self):
        for part in self.parts:
            part.finish()


class Scatter:
    def __init__(self, place, src, slots, send, recv, out):
        self.out = out
        self.cols = halves(src.shape[-1])
        self.parts = [
            ScatterHalf(place, src, self.cols[h], slots[4 * h : 4 * h + 4], ORDERS[h], send, recv, h)
            for h in range(2)
        ]

    def step(self, stage):
        for part, cols in zip(self.parts, self.cols):
            if stage == 4:
                self.out(cols, part.result())
                continue
            if stage:
                part.combine(stage - 1)
            part.launch(stage)

    def finish(self):
        for part in self.parts:
            part.finish()


def slot_shapes(sizes, rows, cols):
    shapes = []
    for order in ORDERS:
        left = [0, 1, 2, 3]
        for dim in (3,) + tuple(order[::-1]):
            left.remove(dim)
            shapes.append((sizes[dim] - 1,) + tuple(sizes[d] for d in left) + (rows, cols // 2))
    return shapes


def head_masks(value):
    row = lax.broadcasted_iota(jnp.int32, (4 * QB, GROUP), 0) // QB
    col = lax.broadcasted_iota(jnp.int32, (4 * QB, GROUP), 1) // HEAD_DIM
    return jnp.where(row == col, value, 0.0).astype(BF16)


def stack_heads(block, mask):
    return jnp.concatenate([block] * 4, axis=0) * mask


def pick_heads(stacked):
    col = lax.broadcasted_iota(jnp.int32, (QB, GROUP), 1) // HEAD_DIM
    parts = [stacked[h * QB : (h + 1) * QB] for h in range(4)]
    return jnp.where(
        col < 2,
        jnp.where(col == 0, parts[0], parts[1]),
        jnp.where(col == 2, parts[2], parts[3]),
    )


def score_bias(step, long_end, short_end):
    row = step * QB + lax.broadcasted_iota(jnp.int32, (QB, 2 * QB), 0)
    key = (step - 1) * QB + lax.broadcasted_iota(jnp.int32, (QB, 2 * QB), 1)
    past = (row - long_end).astype(F32)
    number = jnp.floor((past + 0.5) * (1.0 / SHORT_LEN)).astype(jnp.int32)
    begin = jnp.where(
        row < long_end,
        step * QB,
        jnp.where(row < short_end, long_end + number * SHORT_LEN, row),
    )
    return jnp.where((key >= begin) & (key <= row), 0.0, -1e30)


def row_block(step, count=1):
    return pl.ds(pl.multiple_of(step * QB, QB), count * QB)


def columns(i, size, offset=0):
    return pl.ds(pl.multiple_of(offset + i * size, 128), size)


def group_columns(g):
    return [columns(3 * g + part, GROUP) for part in range(3)]


def attend_steps(g, first, count, qkv_ref, probs_ref, att_ref, mask, long_end, short_end):
    query_cols, key_cols, value_cols = group_columns(g)
    work = []
    for step in [first + u for u in range(count)]:
        bias = score_bias(step, long_end, short_end)
        bias = jnp.concatenate([bias] * 4, axis=0)
        query = stack_heads(qkv_ref[row_block(step + 1), query_cols], mask)
        keys = qkv_ref[row_block(step, 2), key_cols]
        work.append((step, dot_t(query, keys) + bias))
    done = []
    for step, scores in work:
        weight = jnp.exp(scores - jnp.max(scores, axis=-1, keepdims=True))
        total = jnp.sum(weight, axis=-1, keepdims=True)
        probs = (weight * pl.reciprocal(total)).astype(BF16)
        probs_ref[g, step] = probs
        done.append((step, probs))
    for step, probs in done:
        values = qkv_ref[row_block(step, 2), value_cols]
        mixed = pick_heads(dot(probs, values))
        att_ref[row_block(step), columns(g, GROUP)] = mixed.astype(BF16)


def attend_back_steps(g, first, count, qkv_ref, probs_ref, grad_ref, back_ref, carry_ref, masks_ref):
    query_cols, key_cols, value_cols = group_columns(g)
    mask, scaled_mask = masks_ref[0], masks_ref[1]
    work = []
    for step in [first + u for u in range(count)]:
        query = stack_heads(qkv_ref[row_block(step + 1), query_cols], scaled_mask)
        keys = qkv_ref[row_block(step, 2), key_cols]
        values = qkv_ref[row_block(step, 2), value_cols]
        grad = stack_heads(grad_ref[row_block(step), columns(g, GROUP)], mask)
        work.append((step, query, keys, grad, dot_t(grad, values)))
    score_grads = []
    for step, _, _, _, prob_grad in work:
        probs = probs_ref[g, step].astype(F32)
        product = probs * prob_grad
        inner = jnp.sum(product, axis=-1, keepdims=True)
        score_grads.append((product - probs * inner).astype(BF16))
    held = [carry_ref[0], carry_ref[1]]
    for (step, query, keys, grad, _), score_grad in zip(work, score_grads):
        query_grad = pick_heads(dot(score_grad, keys)) * HEAD_DIM ** (-0.5)
        back_ref[row_block(step + 1), query_cols] = query_grad.astype(BF16)
        both = (t_dot(score_grad, query), t_dot(probs_ref[g, step], grad))
        for part, (cols, grads) in enumerate(zip((key_cols, value_cols), both)):
            back_ref[row_block(step), cols] = (held[part] + grads[:QB]).astype(BF16)
            held[part] = grads[QB:]
    for part in range(2):
        carry_ref[part] = held[part]


GATHER_PLAN = {
    "start": {0: ("aux0", "a0", "b0", "aux1", "out0", "a1", "up00", "aux2", "b1", "up10", "aux3", "a2", "out1", "aux4")},
    "norm": {1: ("down00", "b2"), 2: ("up01", "a3")},
    "qkv_a": {0: ("down10", "out2", "up11", "a4"), 2: ("b3", "hid0")},
    "attend_a": {1: ("up02", "down01"), 2: ("logit0",), 3: ("out3",), 4: ("down11",)},
    "qkv_b": {0: ("b4",), 1: ("up12",), 2: ("hid1",)},
    "attend_b": {1: ("up03",), 3: ("down02", "logit1")},
    "out": {0: ("out4",), 2: ("down12",)},
    "up": {0: ("up04",), 1: ("up13",), 2: ("up14", "hid2"), 3: ("down03",), 4: ("logit2",)},
    "down": {0: ("down04",), 1: ("down13",), 2: ("down14",), 3: ("hid3",), 4: ("logit3",)},
    "head": {0: ("hid4", "logit4")},
}
SCATTER_PLAN = {
    "sums": {0: ("logit0", "hid0")},
    "up_back": {1: ("logit1", "hid1")},
    "down_grad": {2: ("logit2", "hid2", "down0")},
    "norm_back": {1: ("logit3", "hid3", "down1")},
    "up_grad": {2: ("down2", "up0")},
    "out_back": {1: ("logit4", "hid4"), 2: ("up1",)},
    "out_grad": {0: ("out0",)},
    "back_a": {1: ("out1", "down3")},
    "grad_a": {0: ("a0",)},
    "back_b": {1: ("up2",), 2: ("a1", "out2"), 4: ("down4",)},
    "grad_b": {0: ("up3", "b0")},
    "token": {1: ("b1",), 2: ("a2", "out3")},
    "end": {0: ("b2", "a3", "out4", "up4", "b3", "a4", "b4")},
}


def layer_kernel(sizes, *refs):
    (
        counts, gain_one_in, gain_two_in, returns_in,
        tokens_hbm, qkv_in, out_in, up_in, down_in, hid_in, logit_in, frames_cot, logits_cot,
        frames_hbm, act_hbm, logit_hbm, grad_hbm, qkv_hbm, norm_hbm, inv_hbm,
        o_qkv, o_out, o_up, o_down, o_hid, o_logit, o_one, o_two,
        norm_ref, inv_ref, att_ref, back_ref, frames_ref, probs_ref, wide_a, wide_b,
        masks_ref, carry_ref, own_up, own_qkv,
        *rest,
    ) = refs
    bufs, rest = rest[:7], rest[7:]
    g_qkv, rest = rest[0], rest[1:]
    slots, rest = [rest[8 * i : 8 * i + 8] for i in range(7)], rest[56:]
    g_sems, rest = [rest[2 * i : 2 * i + 2] for i in range(10)], rest[20:]
    s_sems, rest = [rest[2 * i : 2 * i + 2] for i in range(7)], rest[14:]
    own_sem, in_sem, out_sem, cot_sem = rest
    aux_buf, qkv_buf, out_buf, up_buf, down_buf, hid_buf, logit_buf = bufs

    place = Place(sizes)
    rows, width = back_ref.shape
    hidden = up_buf.shape[-1]
    three = 3 * width
    tile = 512
    tall = 1024
    long_end = counts[0, 0] * LONG_LEN
    short_end = long_end + counts[0, 1] * SHORT_LEN

    def at(i, size=tile, offset=0):
        return pl.ds(pl.multiple_of(offset + i * size, QB), size)

    def start(src, dst, sem):
        copy = pltpu.make_async_copy(src, dst, sem)
        copy.start()
        return copy

    def whole(buf):
        return buf[...].reshape(-1, buf.shape[-1])

    def put(ref):
        def store_out(cols, value):
            ref[:, cols] = value

        return store_out

    def put_group(g):
        def store_out(cols, value):
            first = cols.start
            while first < cols.stop:
                last = min(cols.stop, (first // GROUP + 1) * GROUP)
                to = first // GROUP * 2 * GROUP + GROUP * g + first % GROUP
                o_qkv[:, to : to + last - first] = value[:, first - cols.start : last - cols.start]
                first = last

        return store_out

    def buffers(*pairs):
        return {
            name: Gather(place, buf, first, cols, *g_sems[i])
            for i, (name, buf, first, cols) in enumerate(pairs)
        }

    gathers = buffers(
        ("aux", aux_buf, 0, 128),
        ("a", qkv_buf.at[0], 0, 3 * GROUP),
        ("b", qkv_buf.at[1], 0, 3 * GROUP),
        ("out", out_buf, 0, width),
        ("up0", up_buf, 0, hidden // 2),
        ("up1", up_buf, hidden // 2, hidden // 2),
        ("down0", down_buf, 0, width // 2),
        ("down1", down_buf, width // 2, width // 2),
        ("hid", hid_buf, 0, hid_buf.shape[-1]),
        ("logit", logit_buf, 0, logit_buf.shape[-1]),
    )
    scatters = {
        name: Scatter(place, src, slots[i], *s_sems[i], out)
        for i, (name, src, out) in enumerate((
            ("logit", logit_buf, put(o_logit)),
            ("hid", hid_buf, put(o_hid)),
            ("down", down_buf, put(o_down)),
            ("up", up_buf, put(o_up)),
            ("out", out_buf, put(o_out)),
            ("a", g_qkv.at[0], put_group(0)),
            ("b", g_qkv.at[1], put_group(1)),
        ))
    }

    def transfers(*phases, group=0):
        hooks = []
        for g, phase in enumerate(phases):
            turns = {}
            for plan, items in ((GATHER_PLAN, gathers), (SCATTER_PLAN, scatters)):
                for turn, steps in plan.get(phase, {}).items():
                    turns.setdefault(turn, []).extend((items[s[:-1]], int(s[-1])) for s in steps)

            def run(steps):
                for item, stage in steps:
                    item.step(stage)

            for turn, steps in turns.items():
                hook = functools.partial(run, steps)
                if turn:
                    hooks.append((turn, True if len(phases) == 1 else group == g, hook))
                elif len(phases) == 1:
                    hook()
                else:
                    pl.when(group == g)(hook)
        return hooks

    own = []
    for g in range(2):
        for part in range(3):
            first = 2 * GROUP * part + GROUP * g
            target = qkv_buf.at[(g, *place.digit, slice(None), slice(GROUP * part, GROUP * (part + 1)))]
            own.append(start(qkv_in.at[:, first : first + GROUP], target, own_sem.at[len(own)]))
    for src, buf in ((out_in, out_buf), (up_in, up_buf), (down_in, down_buf), (hid_in, hid_buf), (logit_in, logit_buf)):
        own.append(start(src, buf.at[tuple(place.digit)], own_sem.at[len(own)]))
    own.append(start(up_in, own_up, own_sem.at[11]))
    own.append(start(qkv_in, own_qkv, own_sem.at[12]))
    aux_buf[tuple(place.digit)] = own_block(place, gain_one_in, gain_two_in, returns_in)
    masks_ref[0] = head_masks(1.0)
    masks_ref[1] = head_masks(HEAD_DIM ** (-0.5))
    place.barrier()
    for copy in own:
        copy.wait()

    def gains():
        aux = jnp.sum(aux_buf[...].reshape(-1, *aux_buf.shape[-2:]), axis=0)
        return gain_row(aux, 0), gain_row(aux, 4), place.count / aux[8:9, 0:1]

    def norm_gradient(i, size, grad, gain):
        normed = norm_ref[at(i, size), :].astype(F32) * (1.0 / gain)
        back_ref[at(i, size), :] += norm_back(grad, normed, inv_ref[at(i, size), 0:1], gain)

    def forward(tokens):
        tokens_copy = start(tokens_hbm, tokens, in_sem.at[0])
        transfers("start")
        gain_one, gain_two, _ = gains()
        tokens_copy.wait()

        def norm_tile(i):
            normed, inv_std = normalize(tokens[at(i, tall), :].astype(F32))
            norm_ref[at(i, tall), :] = (normed * gain_one).astype(BF16)
            inv_ref[at(i, tall), :] = jnp.broadcast_to(inv_std, (tall, inv_ref.shape[1]))

        loop(rows // tall, norm_tile, transfers("norm"))
        start(norm_ref, norm_hbm, out_sem.at[6])
        start(inv_ref, inv_hbm, out_sem.at[7])
        wide_a[0:QB, 0:three] = jnp.zeros((QB, three), BF16)

        def group(g):
            hooks = transfers("qkv_a", "qkv_b", group=g)
            cols = columns(g, 3 * GROUP)

            def qkv_tile(i):
                weight = qkv_buf[g].reshape(width, -1)
                wide_a[at(i, tall, QB), cols] = dot(norm_ref[at(i, tall), :], weight).astype(BF16)

            loop(rows // tall, qkv_tile, hooks)

            @pl.when(g == 1)
            def _():
                start(wide_a.at[:, 0:three], qkv_hbm, out_sem.at[0])

            def attend(i):
                attend_steps(g, i * BATCH, BATCH, wide_a, probs_ref, att_ref, masks_ref[1], long_end, short_end)

            loop(rows // QB // BATCH, attend, transfers("attend_a", "attend_b", group=g))

        loop(2, group)
        pltpu.make_async_copy(norm_ref, norm_hbm, out_sem.at[6]).wait()
        pltpu.make_async_copy(inv_ref, inv_hbm, out_sem.at[7]).wait()
        hooks = transfers("out")

        def out_tile(i):
            residual = tokens[at(i), :].astype(F32) + dot(att_ref[at(i), :], whole(out_buf))
            back_ref[at(i), :] = residual
            normed, inv_std = normalize(residual)
            norm_ref[at(i), :] = (normed * gain_two).astype(BF16)
            inv_ref[at(i), :] = jnp.broadcast_to(inv_std, (tile, inv_ref.shape[1]))

        loop(rows // tile, out_tile, hooks)

    pl.run_scoped(forward, pltpu.VMEM((rows, width), BF16))
    pltpu.make_async_copy(wide_a.at[:, 0:three], qkv_hbm, out_sem.at[0]).wait()

    def feed_forward(fcot, lcot, ha_ref, sum_logit, sum_hid):
        _, gain_two, inverse_scale = gains()

        def cotangents(i, slot):
            return [
                pltpu.make_async_copy(frames_cot.at[at(i), :], fcot.at[slot], cot_sem.at[0, slot]),
                pltpu.make_async_copy(logits_cot.at[at(i), :], lcot.at[slot], cot_sem.at[1, slot]),
            ]

        for copy in cotangents(0, 0):
            copy.start()
        hooks = transfers("up")

        def up_tile(i):
            rows_at = at(lax.rem(i, 2), tall)
            for part in range(2):
                cols = columns(2 * (i // 2) + part, hidden // 4)
                value = dot(norm_ref[rows_at, :], up_buf[..., cols].reshape(width, -1))
                slope = jnp.exp(jnp.minimum(value, 0.0))
                wide_b[rows_at, cols] = slope.astype(BF16)
                wide_a[rows_at, cols] = jnp.where(value > 0, value, slope - 1.0).astype(BF16)

        loop(2 * rows // tall, up_tile, hooks)
        hooks = transfers("down")

        def down_tile(i):
            rows_at = at(lax.rem(i, 2), tall)
            cols = columns(i // 2, width // 2)
            value = dot(wide_a[rows_at, 0:hidden], down_buf[..., cols].reshape(hidden, -1))
            frames_ref[rows_at, cols] = (back_ref[rows_at, cols] + value).astype(BF16)

        loop(2 * rows // tall, down_tile, hooks)
        frames_copy = start(frames_ref, frames_hbm, out_sem.at[1])
        transfers("head")
        logit_copy = start(logit_buf, logit_hbm, out_sem.at[8])
        for item in gathers.values():
            item.finish()
        sum_logit[...] = jnp.zeros_like(sum_logit)
        sum_hid[...] = jnp.zeros_like(sum_hid)
        frames_copy.wait()

        def head_tile(i):
            slot = lax.rem(i, 2)

            @pl.when(i + 1 < rows // tile)
            def _():
                for copy in cotangents(i + 1, lax.rem(i + 1, 2)):
                    copy.start()

            for copy in cotangents(i, slot):
                copy.wait()
            row = i * tile + lax.broadcasted_iota(jnp.int32, (tile, 1), 0)
            live = jnp.where(row < short_end, 1.0, 0.0)
            logit_back = (lcot[slot].astype(F32) * (live * inverse_scale)).astype(BF16)
            head_in = frames_ref[at(i), :]
            hidden_rows = dot(head_in, whole(hid_buf))
            act_back = dot_t(logit_back, whole(logit_buf))
            slope = jnp.exp(jnp.minimum(hidden_rows, 0.0))
            hidden_act = jnp.where(hidden_rows > 0, hidden_rows, slope - 1.0).astype(BF16)
            hidden_back = (act_back * slope).astype(BF16)
            ha_ref[at(i), :] = hidden_act
            sum_logit[...] += t_dot(hidden_act, logit_back)
            stream_back = fcot[slot].astype(F32) * live + dot_t(hidden_back, whole(hid_buf))
            sum_hid[...] += t_dot(head_in, hidden_back)
            back_ref[at(i), :] = stream_back
            frames_ref[at(i), :] = stream_back.astype(BF16)

        loop(rows // tile, head_tile)
        act_copy = start(ha_ref, act_hbm, out_sem.at[9])
        logit_copy.wait()
        logit_buf[...] = sum_logit[...].astype(BF16).reshape(logit_buf.shape)
        hid_buf[...] = sum_hid[...].astype(BF16).reshape(hid_buf.shape)
        transfers("sums")

        def up_back_tile(i):
            for part in range(4):
                cols = slice(part * hidden // 4, (part + 1) * hidden // 4)
                grad = dot_t(frames_ref[at(i, tall), :], whole(down_buf)[cols])
                slope = wide_b[at(i, tall), cols].astype(F32)
                wide_b[at(i, tall), cols] = (grad * slope).astype(BF16)

        loop(rows // tall, up_back_tile, transfers("up_back"))
        act_copy.wait()


        def down_grad(i):
            count = sizes[0] // 2
            grad = t_dot(wide_a[0:rows, columns(i, hidden // 2)], frames_ref[...])
            down_buf[pl.ds(i * count, count)] = grad.astype(BF16).reshape((count,) + down_buf.shape[1:])

        loop(2, down_grad, transfers("down_grad"))
        start(qkv_hbm, wide_a.at[:, 0:three], in_sem.at[1])

        def norm_back_tile(i):
            grad = dot_t(wide_b[at(i, tall), 0:hidden], whole(up_buf))
            norm_gradient(i, tall, grad, gain_two)

        loop(rows // tall, norm_back_tile, transfers("norm_back"))

        def up_grad(i):
            cols = columns(i, hidden // 2)
            grad = t_dot(norm_ref[...], wide_b[0:rows, cols])
            up_buf[..., cols] = grad.astype(BF16).reshape(up_buf.shape[:-1] + (-1,))

        loop(2, up_grad, transfers("up_grad"))
        start(norm_hbm, norm_ref, in_sem.at[2])
        start(inv_hbm, inv_ref, in_sem.at[3])

    pl.run_scoped(
        feed_forward,
        pltpu.VMEM((2, tile, frames_cot.shape[1]), BF16),
        pltpu.VMEM((2, tile, logits_cot.shape[1]), BF16),
        pltpu.VMEM((rows, width), BF16),
        pltpu.VMEM((width, logits_cot.shape[1]), F32),
        pltpu.VMEM((width, width), F32),
    )

    gain_one, _, _ = gains()

    def out_back_tile(i):
        out_back = back_ref[at(i, tall), :].astype(BF16)
        frames_ref[at(i, tall), :] = dot_t(out_back, whole(out_buf)).astype(BF16)

    loop(rows // tall, out_back_tile, transfers("out_back"))
    grad = t_dot(att_ref[...], back_ref[...].astype(BF16))
    out_buf[...] = grad.astype(BF16).reshape(out_buf.shape)
    transfers("out_grad")
    pltpu.make_async_copy(qkv_hbm, wide_a.at[:, 0:three], in_sem.at[1]).wait()
    pltpu.make_async_copy(norm_hbm, norm_ref, in_sem.at[2]).wait()
    pltpu.make_async_copy(inv_hbm, inv_ref, in_sem.at[3]).wait()

    def group_back(g):
        carry_ref[...] = jnp.zeros_like(carry_ref)

        def attend_back(i):
            attend_back_steps(g, i * BATCH, BATCH, wide_a, probs_ref, frames_ref, wide_b, carry_ref, masks_ref)

        loop(rows // QB // BATCH, attend_back, transfers("back_a", "back_b", group=g))
        for part, cols in enumerate(group_columns(g)[1:]):
            wide_b[rows : rows + QB, cols] = carry_ref[part].astype(BF16)
        grad = t_dot(norm_ref[...], wide_b[QB : QB + rows, columns(g, 3 * GROUP)])
        g_qkv[g] = grad.astype(BF16).reshape(g_qkv.shape[1:])
        transfers("grad_a", "grad_b", group=g)

    loop(2, group_back)
    hooks = transfers("token")

    def token_tile(i):
        grad = dot_t(wide_b[at(i, offset=QB), 0 : 3 * GROUP], qkv_buf[0].reshape(width, -1))
        grad += dot_t(wide_b[at(i, offset=QB), 3 * GROUP : three], qkv_buf[1].reshape(width, -1))
        norm_gradient(i, tile, grad, gain_one)
        frames_ref[at(i), :] = back_ref[at(i), :].astype(BF16)
        start(frames_ref.at[at(i), :], grad_hbm.at[at(i), :], out_sem.at[2 + i])

    loop(rows // tile, token_tile, hooks)
    transfers("end")
    o_two[...] = gain_grad(o_up, own_up, gain_two_in)
    o_one[...] = gain_grad(o_qkv, own_qkv, gain_one_in)
    for item in scatters.values():
        item.finish()
    for i in range(rows // tile):
        pltpu.make_async_copy(frames_ref.at[at(i), :], grad_hbm.at[at(i), :], out_sem.at[2 + i]).wait()


def own_block(place, gain_one, gain_two, returns):
    own = gain_one.shape[1]
    row = lax.broadcasted_iota(jnp.int32, (4, 128), 0)
    lane = lax.broadcasted_iota(jnp.int32, (4, 128), 1)
    mine = (row * 128 + lane) // own == place.me
    pick_row = lax.broadcasted_iota(jnp.int32, (own, 128), 0)
    pick_lane = lax.broadcasted_iota(jnp.int32, (own, 128), 1)
    pick = jnp.where(lax.rem(pick_lane, own) == pick_row, 1.0, 0.0).astype(BF16)
    spread = [
        jnp.where(mine, jnp.broadcast_to(dot(gain[...], pick), (4, 128)), 0.0)
        for gain in (gain_one, gain_two)
    ]
    time = lax.broadcasted_iota(jnp.int32, returns.shape, 0) * returns.shape[1]
    time = time + lax.broadcasted_iota(jnp.int32, returns.shape, 1)
    steps_back = (returns.shape[0] * returns.shape[1] - 1 - time).astype(F32)
    decays = 0.01 * jnp.exp(steps_back * math.log(0.99))
    terms = jnp.sum(returns[...].astype(F32) * decays, axis=0, keepdims=True)
    mean = jnp.sum(terms, axis=1, keepdims=True)
    return jnp.concatenate(spread + [jnp.broadcast_to(mean, (8, 128))], axis=0)


def gain_grad(weight_grad, weight, gain):
    product = weight_grad[...] * weight[...].astype(F32)
    ones = jnp.ones((8, product.shape[1]), F32)
    total = lax.dot_general(
        ones, product, (((1,), (1,)), ((), ())),
        precision=lax.Precision.HIGHEST, preferred_element_type=F32,
    )
    return total[0:1] / gain[...].astype(F32)


def shape(dims, dtype):
    return jax.ShapeDtypeStruct(tuple(dims), dtype)


def grid_sizes(count):
    chips = count // 2
    return {16: (4, 2, 2, 2), 64: (4, 4, 4, 2)}.get(chips, (chips, 1, 1, 2))


def run_layer(sizes, counts, gains, returns, tokens, weights, frames_cot, logits_cot):
    rows, width = tokens.shape
    qkv_w, out_w, up_w, down_w, hid_w, logit_w = weights
    group = (qkv_w.shape[0], 3 * GROUP)
    blocks = [w.shape for w in (out_w, up_w, down_w, hid_w, logit_w)]
    bufs = [shape(tuple(sizes) + (16, 128), F32), shape((2,) + tuple(sizes) + group, BF16)]
    bufs += [shape(tuple(sizes) + tuple(b), BF16) for b in blocks]
    scatter_blocks = [logit_w.shape, hid_w.shape, down_w.shape, up_w.shape, out_w.shape, group, group]
    slots = [s for block in scatter_blocks for s in slot_shapes(sizes, *block)]
    peers = sum(s - 1 for s in sizes)
    vmem = pl.BlockSpec(memory_space=pltpu.VMEM)
    any_space = pl.BlockSpec(memory_space=pl.ANY)
    own = gains[0].shape[1]
    hidden = up_w.shape[1]
    return pl.pallas_call(
        functools.partial(layer_kernel, sizes),
        out_shape=[
            shape((rows, width), BF16),
            shape((rows, width), BF16),
            bufs[6],
            shape((rows, width), BF16),
            shape((rows + QB, 3 * width), BF16),
            shape((rows, width), BF16),
            shape((rows, 128), F32),
            *[shape(w.shape, F32) for w in weights],
            shape((1, own), F32),
            shape((1, own), F32),
        ],
        in_specs=[pl.BlockSpec(memory_space=pltpu.SMEM)] + [vmem] * 3 + [any_space] * 9,
        out_specs=[any_space] * 7 + [vmem] * 8,
        scratch_shapes=[
            pltpu.VMEM((rows, width), BF16),
            pltpu.VMEM((rows, 128), F32),
            pltpu.VMEM((rows, width), BF16),
            pltpu.VMEM((rows, width), F32),
            pltpu.VMEM((rows, width), BF16),
            pltpu.VMEM((2, rows // QB, 4 * QB, 2 * QB), BF16),
            pltpu.VMEM((rows + QB, hidden), BF16),
            pltpu.VMEM((rows + QB, hidden), BF16),
            pltpu.VMEM((2, 4 * QB, GROUP), BF16),
            pltpu.VMEM((2, QB, GROUP), F32),
            pltpu.VMEM(up_w.shape, BF16),
            pltpu.VMEM(qkv_w.shape, BF16),
            *[pltpu.VMEM(b.shape, b.dtype) for b in bufs],
            pltpu.VMEM(bufs[1].shape, BF16),
            *[pltpu.VMEM(s, BF16) for s in slots],
            *[pltpu.SemaphoreType.DMA((2, peers))] * 34,
            pltpu.SemaphoreType.DMA((13,)),
            pltpu.SemaphoreType.DMA((4,)),
            pltpu.SemaphoreType.DMA((10,)),
            pltpu.SemaphoreType.DMA((2, 2)),
        ],
        compiler_params=pltpu.CompilerParams(
            collective_id=0, has_side_effects=True, vmem_limit_bytes=VMEM_LIMIT
        ),
    )(counts, *gains, returns, tokens, *weights, frames_cot, logits_cot)


def finish_kernel(act_hbm, weight_hbm, *refs):
    count = (len(refs) - 5) // 3
    sources, logits_hbm, targets = refs[:count], refs[count], refs[count + 1 : 2 * count + 1]
    act, weight, wide, logits, *held = refs[2 * count + 1 : -2]
    in_sem, out_sem = refs[-2:]
    tile = act.shape[0] // 4
    jobs = []

    def load(src, dst):
        copy = pltpu.make_async_copy(src, dst, in_sem.at[len(jobs)])
        copy.start()
        jobs.append(copy)
        return copy

    first = load(weight_hbm, weight)
    moves = []
    for i in range(4):
        part = slice(i * tile, (i + 1) * tile)
        moves.append((load(act_hbm.at[part], act.at[part]), logits, logits_hbm, part))
        for src, via, dst in zip(sources[:2], held, targets):
            moves.append((load(src.at[part], via.at[part]), via, dst, part))
    for src, via, dst in zip(sources[2:], held[2:], targets[2:]):
        moves.append((load(src, via), via, dst, slice(None)))
    stores = []
    first.wait()
    for copy, via, dst, part in moves:
        copy.wait()
        if via is logits:
            logits[part] = dot(act[part], weight[...]).astype(BF16)
        if via is held[1]:
            wide[part] = via[part].astype(F32)
            via = wide
        store = pltpu.make_async_copy(via.at[part], dst.at[part], out_sem.at[len(stores)])
        store.start()
        stores.append(store)
    for store in stores:
        store.wait()


def run_finish(act, weight, arrays):
    logits = shape((act.shape[0], weight.shape[1]), BF16)
    any_space = pl.BlockSpec(memory_space=pl.ANY)
    wide = shape(arrays[1].shape, F32)
    outs = [logits, arrays[0], wide, *arrays[2:]]
    held = [logits, *arrays]
    jobs = 13 + len(arrays) - 2
    return pl.pallas_call(
        finish_kernel,
        in_specs=[any_space] * (2 + len(arrays)),
        out_specs=[any_space] * len(outs),
        out_shape=[shape(a.shape, a.dtype) for a in outs],
        scratch_shapes=[
            *[pltpu.VMEM(a.shape, a.dtype) for a in (act, weight, wide, *held)],
            pltpu.SemaphoreType.DMA((jobs,)),
            pltpu.SemaphoreType.DMA((jobs,)),
        ],
        compiler_params=pltpu.CompilerParams(vmem_limit_bytes=VMEM_LIMIT),
    )(act, weight, *arrays)


def shards(
    sizes,
    tokens,
    seq_counts,
    returns,
    ln1_gain,
    qkv_weight,
    out_weight,
    ln2_gain,
    up_weight,
    down_weight,
    prior_hidden_weight,
    prior_logit_weight,
    frames_cot,
    logits_cot,
):
    own = ln1_gain.shape[0]
    (
        frames, act, w_logit, tokens_grad, _, _, _,
        o_qkv, o_out, o_up, o_down, o_hid, o_logit, o_one, o_two,
    ) = run_layer(
        sizes, seq_counts, (ln1_gain.reshape(1, own), ln2_gain.reshape(1, own)), returns.reshape(-1, 128),
        tokens, (qkv_weight, out_weight, up_weight, down_weight, prior_hidden_weight, prior_logit_weight),
        frames_cot, logits_cot,
    )
    logits, frames, tokens_grad, o_qkv, o_out, o_up, o_down, o_hid, o_logit = run_finish(
        act, w_logit.reshape(-1, w_logit.shape[-1]),
        (frames, tokens_grad, o_qkv, o_out, o_up, o_down, o_hid, o_logit),
    )
    return (
        frames, logits, tokens_grad, o_one.reshape(own), o_qkv, o_out, o_two.reshape(own),
        o_up, o_down, o_hid, o_logit,
    )


def solution(mesh):
    sizes = grid_sizes(mesh.shape["fsdp"])
    row = P("fsdp", None)
    vector = P("fsdp")
    return jax.shard_map(
        functools.partial(shards, sizes),
        mesh=mesh,
        in_specs=(row, row, vector, vector, row, row, vector, row, row, row, row, row, row),
        out_specs=(row, row, row, vector, row, row, vector, row, row, row, row),
        check_vma=False,
    )
```
